32 devices in a mesh: row: 4 (over y, core), col: 8 (over z, x).
Axes of the slice: x: 2, y: 2, z: 4, core: 2. Of those that a mesh axis runs over, the one named last changes fastest.
Arguments:
- prolong: bfloat16 [6144, 2048], P('col', 'row'), may hold values from -0.21875 to 0.21875
- applied: bfloat16 [6144, 2048], P('row', 'col'), may hold values from -6 to 6
- prolong_pattern: int32 [48, 16], P('col', 'row'), may hold values from 0 to 1, as said below
- applied_pattern: int32 [48, 16], P('row', 'col'), may hold values from 0 to 1, as said below
Outputs:
- coarse_operator: float32 [2048, 2048], P('row', 'col')
The draws below stay inside these ranges and needn't reach their ends.
Inputs may be any that keep to these rules, and one draw needn't show every extreme that they name: In each fine tile row a, the nonzero tiles of prolong_pattern are one run of 1 to 3 consecutive coarse tiles that holds tile a * 16 // 48 (cut at the ends of the range), and the tile (a * 16 // 48 + 16 // 2) mod 16. In each fine tile row a, the nonzero tiles of applied_pattern are one run of 3 to 5 consecutive coarse tiles that holds tile a * 16 // 48 (cut at the ends of the range), and the tile (a * 16 // 48 + 16 // 2) mod 16.
All inputs are finite; a program needn't handle non-finite values.
Results may differ from the reference program's by a relative error of at most 0.0003.
Values may be sent and summed in bfloat16 or wider, within the bound.
No kernel may reach another device: no remote copies, remote signals or barrier semaphores. Data moves between devices by JAX's collectives and lax.ppermute only.
A program may use at most 64 MiB of HBM per device.

```python
import jax
import jax.numpy as jnp
from jax import lax

TILE = 128
NCT = 16
NFT = 48
NC = 2048
NF = 6144


def band_pattern(key, reach_low, reach_high):
    first_key, second_key = jax.random.split(key)
    fine_rows = jnp.arange(NFT, dtype=jnp.int32)
    centre = fine_rows * NCT // NFT
    lower_reach = jax.random.randint(first_key, (NFT,), reach_low, reach_high, dtype=jnp.int32)
    upper_reach = jax.random.randint(second_key, (NFT,), reach_low, reach_high, dtype=jnp.int32)
    columns = jnp.arange(NCT, dtype=jnp.int32)[None, :]
    offset = columns - centre[:, None]
    inside = (offset >= -lower_reach[:, None]) & (offset <= upper_reach[:, None])
    far_tile = (centre + NCT // 2) % NCT
    inside = inside | (columns == far_tile[:, None])
    return jnp.where(inside, 1, 0).astype(jnp.int32)


def draw_prolong_pattern(key, part):
    return band_pattern(jax.random.fold_in(key, 11), 0, 2)


def draw_applied_pattern(key, part):
    return band_pattern(jax.random.fold_in(key, 23), 1, 3)


def levels(rng, shape, cuts, least, largest):
    factor_of = 1.0
    for position, blocks in cuts:
        draws = jax.random.uniform(jax.random.fold_in(jax.random.fold_in(rng, 6), position), (blocks,), jnp.float32, least / len(cuts), largest / len(cuts))
        factor_of = factor_of * jnp.repeat(jnp.exp(draws), shape[position] // blocks).reshape((-1,) + (1,) * (len(shape) - 1 - position))
    return factor_of


def bell_draw(own_key, shape, deviation, limit, cuts=(), kind=jnp.bfloat16):
    entries = jax.random.normal(own_key, shape, jnp.float32) * deviation
    if len(cuts) > 0:
        entries = levels(own_key, shape, cuts, -0.22, 0.18) * entries
    return jnp.clip(entries, min=-limit, max=limit).astype(kind)


def setup_inputs(seed: int = 0) -> dict:
    arg_keys = jax.random.split(jax.random.key(seed), 5)
    return {
        "prolong": bell_draw(arg_keys[0], (NF, NC), (2 * TILE * NFT // NCT) ** -0.5, 0.21875, ((0, 8), (1, 4))),
        "applied": bell_draw(arg_keys[1], (NF, NC), 1.0, 6.0, ((0, 4), (1, 8))),
        "prolong_pattern": draw_prolong_pattern(jax.random.fold_in(arg_keys[4], 71), 0),
        "applied_pattern": draw_applied_pattern(jax.random.fold_in(arg_keys[4], 71), 0),
    }


def apply_pattern(matrix, pattern):
    height, width = matrix.shape
    tile_rows, tile_cols = pattern.shape
    weights = pattern.astype(matrix.dtype)
    shaped = matrix.reshape(tile_rows, height // tile_rows, tile_cols, width // tile_cols)
    return (shaped * weights[:, None, :, None]).reshape(height, width)


def reference(prolong, applied, prolong_pattern, applied_pattern):
    masked_p = apply_pattern(prolong, prolong_pattern)
    masked_ap = apply_pattern(applied, applied_pattern)
    return lax.dot_general(masked_p, masked_ap, (((0,), (0,)), ((), ())), preferred_element_type=jnp.float32)
```

```python
import functools

import jax
import jax.numpy as jnp
from jax import lax
from jax.experimental import pallas as pl
from jax.experimental.pallas import tpu as pltpu
from jax.sharding import PartitionSpec as P

TILE = 128
AXES = ("row", "col")
OWN, SIDE, IN, OUT, FAR, DIAG_IN, DIAG_OUT = range(7)


def inward(source, cols):
    return source + 2 if source < cols // 2 else source - 2


def outward(source, cols):
    target = source - 2 if source < cols // 2 else source + 2
    return target if 0 <= target < cols else None


def diagonal(source, cols):
    target = source - 1 if source % 2 == 0 else source + 1
    return target if 0 <= target < cols else None


def routes(sources, cols):
    pairs = {kind: [] for kind in (SIDE, IN, OUT, FAR, DIAG_IN, DIAG_OUT)}
    for s in sources:
        pairs[SIDE].append((s, s ^ 1))
        a, b, d = inward(s, cols), outward(s, cols), diagonal(s, cols)
        pairs[IN].append((s, a))
        pairs[FAR].append((a, (s + cols // 2) % cols))
        if b is not None:
            pairs[OUT].append((s, b))
        if d is not None:
            relay = s - 2 if s % 2 == 0 else s + 2
            pairs[DIAG_IN if relay == a else DIAG_OUT].append((relay, d))
    return pairs


def main_sources(r, cols):
    return [2 * r, 2 * r + 1]


def small_sources(r, cols):
    near = [s for s in (2 * r - 1, 2 * r + 2) if 0 <= s < cols]
    return near + [(2 * r + cols // 2) % cols, (2 * r + 1 + cols // 2) % cols]


def all_pairs(sources_of, rows, cols):
    total = {}
    for r in range(rows):
        for kind, pairs in routes(sources_of(r, cols), cols).items():
            assert len({d for _, d in pairs}) == len(pairs)
            assert len({s for s, _ in pairs}) == len(pairs)
            total.setdefault(kind, []).extend((r * cols + s, r * cols + d) for s, d in pairs)
    return total


def spread(block, pairs):
    move = lambda x, kind: lax.ppermute(x, AXES, pairs[kind])
    got = {OWN: block}
    got[IN] = move(block, IN)
    got[SIDE] = move(block, SIDE)
    got[OUT] = move(block, OUT)
    got[FAR] = move(got[IN], FAR)
    got[DIAG_IN] = move(got[IN], DIAG_IN)
    got[DIAG_OUT] = move(got[OUT], DIAG_OUT)
    return [got[kind] for kind in range(7)]


def arrival(source, c, cols):
    diff = c - source
    low = source < cols // 2
    even = source % 2 == 0
    side = jnp.where(even, 1, -1)
    is_in = diff == jnp.where(low, 2, -2)
    is_out = diff == jnp.where(low, -2, 2)
    diag_kind = jnp.where(even == low, DIAG_OUT, DIAG_IN)
    kind = jnp.where(diff == 0, OWN, -1)
    kind = jnp.where(diff == side, SIDE, kind)
    kind = jnp.where(diff == -side, diag_kind, kind)
    kind = jnp.where((diff == cols // 2) | (diff == -(cols // 2)), FAR, kind)
    kind = jnp.where(is_out, OUT, kind)
    kind = jnp.where(is_in, IN, kind)
    return kind


def prepare_kernel(cols, p_ref, ap_ref, pp_ref, app_ref, pm_ref, apm_ref, small_ref):
    r, c = lax.axis_index("row"), lax.axis_index("col")
    fine = p_ref.shape[0] // TILE
    for a in range(fine):
        for b in range(p_ref.shape[1] // TILE):
            at = (pl.ds(a * TILE, TILE), pl.ds(b * TILE, TILE))
            pm_ref[at] = jnp.where(pp_ref[a, b] > 0, p_ref[at], jnp.zeros((TILE, TILE), p_ref.dtype))
    for a in range(ap_ref.shape[0] // TILE):
        for b in range(ap_ref.shape[1] // TILE):
            at = (pl.ds(a * TILE, TILE), pl.ds(b * TILE, TILE))
            apm_ref[at] = jnp.where(app_ref[a, b] > 0, ap_ref[at], jnp.zeros((TILE, TILE), ap_ref.dtype))
    half = p_ref.shape[0] // 2

    def pack(units):
        for u, (m, i) in enumerate(units):
            small_ref[pl.ds(u * half, half), :] = pm_ref[pl.ds(m * half, half), pl.ds(i * TILE, TILE)]

    @pl.when(c == 2 * r - 1)
    def _():
        pack(BEFORE)

    @pl.when(c == 2 * r + 2)
    def _():
        pack(AFTER)

    @pl.when(c == lax.rem(2 * r + cols // 2, cols))
    def _():
        pack(FAR_FIRST)

    @pl.when(c == lax.rem(2 * r + 1 + cols // 2, cols))
    def _():
        pack(FAR_SECOND)


BEFORE = ((0, 0), (1, 0), (1, 1))
AFTER = ((0, 2), (0, 3), (1, 3))
FAR_FIRST = ((0, 0), (1, 1))
FAR_SECOND = ((0, 2), (1, 3))


def product(p, ap):
    return lax.dot_general(p, ap, (((0,), (0,)), ((), ())), preferred_element_type=jnp.float32)


def combine_kernel(cols, own_ap, far_ap, core_ap, cross_ap, *refs):
    mains, smalls, c_ref = refs[:7], refs[7:14], refs[14]
    main_scratch, small_scratch = refs[15], refs[16]
    r, c = lax.axis_index("row"), lax.axis_index("col")
    depth = mains[0].shape[0]
    half = depth // 2
    odd = r % 2 == 1
    c_ref[...] = jnp.zeros_like(c_ref)

    def fetch(kind, buffers, scratch):
        for k in range(7):
            @pl.when(kind == k)
            def _(k=k):
                scratch[...] = buffers[k][...]

    for e in range(2):
        kind = arrival(2 * r + e, c, cols)

        @pl.when(kind >= 0)
        def _(kind=kind, e=e):
            fetch(kind, mains, main_scratch)
            c_ref[...] += product(main_scratch[...], own_ap[pl.ds(e * depth, depth), :])

    def small(source, valid, units, ap_rows):
        kind = arrival(source, c, cols)

        @pl.when(valid & (kind >= 0))
        def _():
            fetch(kind, smalls, small_scratch)
            for u, (m, i) in enumerate(units):
                rows = pl.ds(i * TILE, TILE)
                c_ref[rows, :] += product(small_scratch[pl.ds(u * half, half), :], ap_rows(m))

    within = lambda ref, start: (lambda m: ref[pl.ds(start + m * half, half), :])
    small(lax.rem(2 * r + cols // 2, cols), True, FAR_FIRST, within(far_ap, 0))
    small(lax.rem(2 * r + 1 + cols // 2, cols), True, FAR_SECOND, within(far_ap, depth))
    small(2 * r - 1, odd, BEFORE, within(core_ap, 0))
    small(2 * r - 1, (r > 0) & ~odd, BEFORE, within(cross_ap, 0))
    small(2 * r + 2, ~odd, AFTER, within(core_ap, 0))
    small(2 * r + 2, (2 * r + 2 < cols) & odd, AFTER, within(cross_ap, 0))


def on_device(rows, cols, prolong, applied, prolong_pattern, applied_pattern):
    depth = prolong.shape[0]
    half = depth // 2
    vmem = pl.BlockSpec(memory_space=pltpu.VMEM)
    smem = pl.BlockSpec(memory_space=pltpu.SMEM)
    shape = lambda h, w: jax.ShapeDtypeStruct((h, w), prolong.dtype)
    masked_p, masked_ap, small = pl.pallas_call(
        functools.partial(prepare_kernel, cols),
        out_shape=(shape(*prolong.shape), shape(*applied.shape), shape(3 * half, TILE)),
        in_specs=[vmem, vmem, smem, smem],
        out_specs=(vmem, vmem, vmem),
        compiler_params=pltpu.CompilerParams(vmem_limit_bytes=16 << 20),
    )(prolong, applied, prolong_pattern, applied_pattern)

    device = lambda r, c: r * cols + c
    across = [(device(r, c), device((r + rows // 2) % rows, c)) for r in range(rows) for c in range(cols)]
    partner = [(device(r, c), device(r ^ 1, c)) for r in range(rows) for c in range(cols)]
    beyond = [
        (device(r, c), device(t, c))
        for r in range(rows)
        for t in [r + 1 if r % 2 == 1 else r - 1]
        if 0 <= t < rows
        for c in range(cols)
    ]
    odd = lax.axis_index("row") % 2 == 1
    lower, upper = masked_ap[:depth], masked_ap[depth:]
    far_ap = lax.ppermute(masked_ap, AXES, across)
    mains = spread(masked_p, all_pairs(main_sources, rows, cols))
    core_ap = lax.ppermute(jnp.where(odd, lower, upper), AXES, partner)
    cross_ap = lax.ppermute(jnp.where(odd, upper, lower), AXES, beyond)
    smalls = spread(small, all_pairs(small_sources, rows, cols))

    return pl.pallas_call(
        functools.partial(combine_kernel, cols),
        out_shape=jax.ShapeDtypeStruct((prolong.shape[1], applied.shape[1]), jnp.float32),
        in_specs=[vmem] * 18,
        out_specs=vmem,
        scratch_shapes=[pltpu.VMEM(prolong.shape, prolong.dtype), pltpu.VMEM((3 * half, TILE), prolong.dtype)],
        compiler_params=pltpu.CompilerParams(vmem_limit_bytes=32 << 20),
    )(masked_ap, far_ap, core_ap, cross_ap, *mains, *smalls)


def solution(mesh):
    in_specs = (P("col", "row"), P("row", "col"), P("col", "row"), P("row", "col"))
    return jax.shard_map(
        functools.partial(on_device, mesh.shape["row"], mesh.shape["col"]),
        mesh=mesh, in_specs=in_specs, out_specs=P("row", "col"), check_vma=False,
    )
```

```python
import functools

import jax
import jax.numpy as jnp
from jax import lax
from jax.experimental import pallas as pl
from jax.experimental.pallas import tpu as pltpu
from jax.sharding import PartitionSpec as P

TILE = 128
AXES = ("row", "col")
SLOTS = 3
META = 16
MAINS, NEARS, FARS = (0, 1), (2, 3), (4, 5)
UNITS = (
    ((0, 0), (0, 1), (0, 2), (1, 0), (1, 1), (1, 2), (1, 3)),
    ((0, 0), (0, 1), (0, 2), (0, 3), (1, 1), (1, 2), (1, 3)),
    ((0, 0), (1, 0), (1, 1)),
    ((0, 2), (0, 3), (1, 3)),
    ((0, 0), (1, 1)),
    ((0, 2), (1, 3)),
)
OWN, SIDE, UP, DOWN, FAR, DIAG = range(6)
FIRST, SECOND = (SIDE, UP, DOWN), (FAR, DIAG)


def class_sources(r, cols):
    rem = lambda x: lax.rem(x, cols)
    return (2 * r, 2 * r + 1, 2 * r - 1, 2 * r + 2, rem(2 * r + cols // 2), rem(2 * r + 1 + cols // 2))


def kind_sources(c, cols):
    even = c % 2 == 0
    near, past = jnp.where(even, c + 1, c - 1), jnp.where(even, c - 1, c + 1)
    return {OWN: c, SIDE: near, UP: c - 2, DOWN: c + 2, FAR: lax.rem(c + cols // 2, cols), DIAG: past}


def slot_of(name, i, odd, width):
    return 2 if name in FARS else (i + (width if odd else 0)) % SLOTS


def mask_tiles(out_ref, in_ref, pattern_ref, rows):
    for a, row in enumerate(rows):
        for b in range(in_ref.shape[1] // TILE):
            tile = in_ref[pl.ds(row * TILE, TILE), pl.ds(b * TILE, TILE)]
            kept = jnp.where(pattern_ref[b, row] > 0, tile, jnp.zeros_like(tile))
            out_ref[pl.ds(a * TILE, TILE), pl.ds(b * TILE, TILE)] = kept


def prepare_applied(ap_ref, pattern_ref, out_ref):
    odd = lax.axis_index("row") % 2 == 1
    count = ap_ref.shape[0] // TILE
    lower, upper = list(range(count // 2)), list(range(count // 2, count))

    @pl.when(odd)
    def _():
        mask_tiles(out_ref, ap_ref, pattern_ref, upper + lower)

    @pl.when(jnp.logical_not(odd))
    def _():
        mask_tiles(out_ref, ap_ref, pattern_ref, lower + upper)


def prepare_prolong(cols, p_ref, pattern_ref, keep_ref, send_ref):
    r, c = lax.axis_index("row"), lax.axis_index("col")
    tiles = p_ref.shape[0] // TILE // 2
    half = tiles * TILE
    width = p_ref.shape[1] // TILE
    sources = class_sources(r, cols)
    zeros = jnp.zeros((TILE, TILE), p_ref.dtype)
    line = lax.broadcasted_iota(jnp.int32, (META, TILE), 0)

    def pack(name, odd):
        for out_ref, m in ((keep_ref, int(odd)), (send_ref, 1 - int(odd))):
            for s in range(SLOTS):
                found = [i for mm, i in UNITS[name] if mm == m and slot_of(name, i, odd, width) == s]
                for a in range(tiles):
                    value, row = zeros, m * tiles + a
                    for i in found:
                        tile = p_ref[pl.ds(row * TILE, TILE), pl.ds(i * TILE, TILE)]
                        value = jnp.where(pattern_ref[i, row] > 0, tile, value)
                    out_ref[pl.ds(s * half + a * TILE, TILE), :] = value

    def note(odd):
        for out_ref, m in ((keep_ref, int(odd)), (send_ref, 1 - int(odd))):
            value = jnp.zeros((META, TILE), jnp.float32)
            for a in range(tiles):
                for i in range(width):
                    value = jnp.where(line == a * width + i, pattern_ref[i, m * tiles + a].astype(jnp.float32), value)
            out_ref[pl.ds(SLOTS * half, META), :] = value.astype(out_ref.dtype)

    for odd in (False, True):
        parity = (r % 2 == 1) == odd

        @pl.when(parity)
        def _(odd=odd):
            note(odd)

        for name in range(len(UNITS)):
            @pl.when(parity & (c == sources[name]))
            def _(name=name, odd=odd):
                pack(name, odd)

    @pl.when(functools.reduce(jnp.logical_and, [c != s for s in sources]))
    def _():
        for out_ref in (keep_ref, send_ref):
            out_ref[pl.ds(0, SLOTS * half), :] = jnp.zeros((SLOTS * half, TILE), p_ref.dtype)


def merge_kernel(keep_ref, got_ref, half_ref):
    odd = lax.axis_index("row") % 2 == 1
    size = keep_ref.shape[0] - META
    half_ref[pl.ds(0, size), :] = keep_ref[pl.ds(0, size), :] + got_ref[pl.ds(0, size), :]
    mine, theirs = keep_ref[pl.ds(size, META), :], got_ref[pl.ds(size, META), :]
    half_ref[pl.ds(size, META), :] = jnp.where(odd, theirs, mine)
    half_ref[pl.ds(size + META, META), :] = jnp.where(odd, mine, theirs)


def put_columns(out_ref, start, ap):
    rows = ap.shape[0]
    for b in range(ap.shape[1] // TILE):
        out_ref[pl.ds(start + b * rows, rows), :] = ap[:, b * TILE : (b + 1) * TILE]


def forward_kernel(cols, half, side, up, down, ap_ref, far_out, diag_out, swap_out):
    c = lax.axis_index("col")
    relays = cols == 8
    inner_low = relays & (c >= 2) & (c < 4)
    inner_high = relays & (c >= 4) & (c < 6)

    @pl.when(inner_low)
    def _():
        far_out[...] = down[...]

    @pl.when(inner_high)
    def _():
        far_out[...] = up[...]

    @pl.when(jnp.logical_not(inner_low | inner_high))
    def _():
        far_out[...] = half[...]

    @pl.when(c % 2 == 0)
    def _():
        diag_out[...] = down[...]

    @pl.when(c % 2 == 1)
    def _():
        diag_out[...] = up[...]

    size = half.shape[0]
    for j, buffer in enumerate((side, up, down)):
        swap_out[pl.ds(j * size, size), :] = buffer[...]
    depth = ap_ref.shape[0] // 2
    put_columns(swap_out, len(FIRST) * size, ap_ref[pl.ds(depth, depth), :])


def last_swap_kernel(far, diag, far_ap, swap_out):
    size = far.shape[0]
    for j, buffer in enumerate((far, diag)):
        swap_out[pl.ds(j * size, size), :] = buffer[...]
    depth = far_ap.shape[0] // 2
    put_columns(swap_out, len(SECOND) * size, far_ap[pl.ds(0, depth), :])


def product(p, ap):
    return lax.dot_general(p, ap, (((0,), (0,)), ((), ())), preferred_element_type=jnp.float32)


def accumulate(cols, name, valid, buffers, c_ref, block, read_ap, half, width):
    r, c = lax.axis_index("row"), lax.axis_index("col")
    odd = r % 2 == 1
    data = SLOTS * half
    stride = data + META
    source = class_sources(r, cols)[name]
    at = kind_sources(c, cols)
    inside = valid & (source >= 0) & (source < cols)
    here = [inside & (at[kind] == source) for kind in buffers]
    start = {True: pl.multiple_of(jnp.where(odd, stride, 0), META), False: pl.multiple_of(jnp.where(odd, 0, stride), META)}

    @pl.when(functools.reduce(jnp.logical_or, here))
    def _():
        for flag, (kind, (mine, theirs, row)) in zip(here, buffers.items()):
            @pl.when(flag)
            def _(kind=kind, mine=mine, theirs=theirs, row=row):
                for is_mine, ref, base in ((True, mine, 0), (False, theirs, row)):
                    note = data if kind == OWN else pl.multiple_of(data + jnp.where(odd, META, 0), META)
                    block[pl.ds(start[is_mine], data), :] = ref[pl.ds(base, data), :]
                    block[pl.ds(start[is_mine] + data, META), :] = ref[pl.ds(base + note, META), :]
        for m in sorted({m for m, _ in UNITS[name]}):
            pattern = block[pl.ds(m * stride + data, META), :].astype(jnp.float32)
            ap = read_ap(m)
            for i in [i for mm, i in UNITS[name] if mm == m]:
                slot = jnp.where(odd, slot_of(name, i, True, width), slot_of(name, i, False, width))
                first = pl.multiple_of(m * stride + slot * half, META)
                lhs = []
                for a in range(half // TILE):
                    line = a * width + i
                    weight = jnp.broadcast_to(pattern[line : line + 1, :], (TILE, TILE)).astype(block.dtype)
                    lhs.append(block[pl.ds(first + a * TILE, TILE), :] * weight)
                c_ref[pl.ds(i * TILE, TILE), :] += product(jnp.concatenate(lhs, axis=0), ap)


def readers(odd, half, own_ap, core, core_row, far_ap):
    depth = 2 * half

    def in_order(ref, upper):
        row = jnp.where(odd == upper, 0, depth)
        return lambda m: ref[pl.ds(pl.multiple_of(row + m * half, TILE), half), :]

    def columns(ref, start):
        return lambda m: jnp.concatenate([ref[pl.ds(start + b * depth + m * half, half), :] for b in range(2)], axis=1)

    return in_order, columns


def near_kernel(cols, half, width, own_ap, keep, send, side, up, down, swapped, c_ref, block):
    odd = lax.axis_index("row") % 2 == 1
    size = side.shape[0]
    buffers = {OWN: (keep, send, 0)}
    buffers |= {kind: (ref, swapped, j * size) for j, (kind, ref) in enumerate(zip(FIRST, (side, up, down)))}
    in_order, columns = readers(odd, half, own_ap, None, 0, None)
    c_ref[...] = jnp.zeros_like(c_ref)
    for name in MAINS:
        accumulate(cols, name, True, buffers, c_ref, block, in_order(own_ap, name == 1), half, width)
    for name, valid in zip(NEARS, (odd, jnp.logical_not(odd))):
        accumulate(cols, name, valid, buffers, c_ref, block, columns(swapped, len(FIRST) * size), half, width)


def far_kernel(cols, half, width, own_ap, far_ap, keep, send, side, up, down, swapped, far, diag, last, cross, partial, c_ref, block):
    odd = lax.axis_index("row") % 2 == 1
    size = side.shape[0]
    early = {OWN: (keep, send, 0)}
    early |= {kind: (ref, swapped, j * size) for j, (kind, ref) in enumerate(zip(FIRST, (side, up, down)))}
    late = {kind: (ref, last, j * size) for j, (kind, ref) in enumerate(zip(SECOND, (far, diag)))}
    in_order, columns = readers(odd, half, own_ap, None, 0, None)
    c_ref[...] = partial[...]
    for name in MAINS:
        accumulate(cols, name, True, late, c_ref, block, in_order(own_ap, name == 1), half, width)
    for name, valid in zip(NEARS, (odd, jnp.logical_not(odd))):
        accumulate(cols, name, valid, late, c_ref, block, columns(swapped, len(FIRST) * size), half, width)
        cross_row = cross.shape[0] - own_ap.shape[0]
        accumulate(cols, name, jnp.logical_not(valid), early | late, c_ref, block, columns(cross, cross_row), half, width)
    for name in FARS:
        accumulate(cols, name, True, early | late, c_ref, block, in_order(far_ap, name == 5), half, width)


def on_device(rows, cols, prolong, applied, prolong_pattern, applied_pattern):
    depth, width = prolong.shape[0], prolong.shape[1] // TILE
    half = depth // 2
    data = SLOTS * half
    size = data + 2 * META
    vmem = pl.BlockSpec(memory_space=pltpu.VMEM)
    smem = pl.BlockSpec(memory_space=pltpu.SMEM)
    params = pltpu.CompilerParams(vmem_limit_bytes=24 << 20)
    shape = lambda *s: jax.ShapeDtypeStruct(s, prolong.dtype)

    def call(kernel, name, out_shape, *operands, specs=None, **more):
        out_specs = (vmem,) * len(out_shape) if isinstance(out_shape, tuple) else vmem
        return pl.pallas_call(
            kernel, out_shape=out_shape, in_specs=specs or [vmem] * len(operands), out_specs=out_specs,
            compiler_params=params, name=name, **more,
        )(*operands)

    def move(x, pairs):
        return lax.ppermute(x, AXES, pairs)

    def row_pairs(pairs):
        return [(a * cols + c, b * cols + c) for a, b in pairs for c in range(cols)]

    def col_pairs(pairs):
        return [(r * cols + a, r * cols + b) for r in range(rows) for a, b in pairs if 0 <= b < cols]

    partner = row_pairs([(r, r ^ 1) for r in range(rows)])
    opposite = [(r, (r + rows // 2) % rows) for r in range(rows)]

    own_ap = call(prepare_applied, "prepare_applied", shape(*applied.shape), applied, applied_pattern.T, specs=[vmem, smem])
    far_ap = move(own_ap, row_pairs(opposite))
    keep, send = call(
        functools.partial(prepare_prolong, cols), "prepare_prolong", (shape(data + META, TILE),) * 2,
        prolong, prolong_pattern.T, specs=[vmem, smem],
    )
    mine = call(merge_kernel, "merge", shape(size, TILE), keep, move(send, partner))
    side = move(mine, col_pairs([(c, c ^ 1) for c in range(cols)]))
    up = move(mine, col_pairs([(c, c + 2) for c in range(cols)]))
    down = move(mine, col_pairs([(c, c - 2) for c in range(cols)]))

    ap_rows = 2 * depth
    far_send, diag_send, swap = call(
        functools.partial(forward_kernel, cols), "forward",
        (shape(size, TILE), shape(size, TILE), shape(len(FIRST) * size + ap_rows, TILE)), mine, side, up, down, own_ap,
    )
    if cols == 8:
        far_pairs = [(0, 4), (1, 5), (2, 0), (3, 1), (4, 6), (5, 7), (6, 2), (7, 3)]
    else:
        far_pairs = [(c, (c + cols // 2) % cols) for c in range(cols)]
    far = move(far_send, col_pairs(far_pairs))
    diag = move(diag_send, col_pairs([(c, c + 1) for c in range(0, cols - 2, 2)] + [(c, c - 1) for c in range(3, cols, 2)]))
    swapped = move(swap, partner)
    last = move(
        call(last_swap_kernel, "last_swap", shape(len(SECOND) * size + ap_rows, TILE), far, diag, far_ap), partner
    )
    beyond = [(r, r + 1 if r % 2 == 1 else r - 1) for r in range(rows)]
    relay = [((r + rows // 2) % rows, t) for r, t in beyond if 0 <= t < rows]
    if all(h ^ 1 == t for h, t in relay):
        cross = last
    else:
        first = own_ap[:depth].reshape(depth, 2, TILE).transpose(1, 0, 2).reshape(ap_rows, TILE)
        cross = move(first, row_pairs([(r, t) for r, t in beyond if 0 <= t < rows]))

    result = jax.ShapeDtypeStruct((prolong.shape[1], applied.shape[1]), jnp.float32)
    scratch = dict(scratch_shapes=[pltpu.VMEM((2 * (data + META), TILE), prolong.dtype)])
    partial = call(
        functools.partial(near_kernel, cols, half, width), "near", result,
        own_ap, keep, send, side, up, down, swapped, **scratch,
    )
    return call(
        functools.partial(far_kernel, cols, half, width), "far", result,
        own_ap, far_ap, keep, send, side, up, down, swapped, far, diag, last, cross, partial, **scratch,
    )


def solution(mesh):
    in_specs = (P("col", "row"), P("row", "col"), P("col", "row"), P("row", "col"))
    return jax.shard_map(
        functools.partial(on_device, mesh.shape["row"], mesh.shape["col"]),
        mesh=mesh, in_specs=in_specs, out_specs=P("row", "col"), check_vma=False,
    )
```

```python
import functools

import jax
import jax.numpy as jnp
from jax import lax
from jax.experimental import pallas as pl
from jax.experimental.pallas import tpu as pltpu
from jax.sharding import PartitionSpec as P

TILE = 128
AXES = ("row", "col")
LAST_WEIGHT = 20
SLOTS = 3
META = 16
MAINS, NEARS, FARS = (0, 1), (2, 3), (4, 5)
UNITS = (
    ((0, 0), (0, 1), (0, 2), (1, 0), (1, 1), (1, 2), (1, 3)),
    ((0, 0), (0, 1), (0, 2), (0, 3), (1, 1), (1, 2), (1, 3)),
    ((0, 0), (1, 0), (1, 1)),
    ((0, 2), (0, 3), (1, 3)),
    ((0, 0), (1, 1)),
    ((0, 2), (1, 3)),
)
OWN, SIDE, PAIR, CROSS, FAR, DIAG = range(6)
FIRST, SECOND = (SIDE, PAIR, CROSS), (FAR, DIAG)


def class_sources(r, cols):
    rem = lambda x: lax.rem(x, cols)
    return (2 * r, 2 * r + 1, 2 * r - 1, 2 * r + 2, rem(2 * r + cols // 2), rem(2 * r + 1 + cols // 2))


def kind_sources(c, cols):
    even, low = c % 2 == 0, (c // 2) % 2 == 0
    near, past = jnp.where(even, c + 1, c - 1), jnp.where(even, c - 1, c + 1)
    pair, across = jnp.where(low, c + 2, c - 2), jnp.where(low, c - 2, c + 2)
    return {OWN: c, SIDE: near, PAIR: pair, CROSS: across, FAR: lax.rem(c + cols // 2, cols), DIAG: past}


def slot_of(name, i, odd, width):
    return 2 if name in FARS else (i + (width if odd else 0)) % SLOTS


def prepare_kernel(cols, p_hbm, ap_hbm, p_pattern_hbm, ap_pattern_hbm, keep_ref, send_ref, out_ref, p_ref, ap_ref, p_pattern, ap_pattern, sems):
    copies = [
        pltpu.make_async_copy(source, target, sems.at[i])
        for i, (source, target) in enumerate(
            ((p_pattern_hbm, p_pattern), (p_hbm, p_ref), (ap_pattern_hbm, ap_pattern), (ap_hbm, ap_ref))
        )
    ]
    for copy in copies:
        copy.start()
    r, c = lax.axis_index("row"), lax.axis_index("col")
    tiles = p_ref.shape[0] // TILE // 2
    half = tiles * TILE
    width = p_ref.shape[1] // TILE
    sources = class_sources(r, cols)
    zeros = jnp.zeros((TILE, TILE), p_ref.dtype)
    line = lax.broadcasted_iota(jnp.int32, (META, TILE), 0)

    def pack(name, odd):
        for out_ref, m in ((keep_ref, int(odd)), (send_ref, 1 - int(odd))):
            for s in range(SLOTS):
                found = [i for mm, i in UNITS[name] if mm == m and slot_of(name, i, odd, width) == s]
                for a in range(tiles):
                    value, row = zeros, m * tiles + a
                    for i in found:
                        tile = p_ref[pl.ds(row * TILE, TILE), pl.ds(i * TILE, TILE)]
                        value = jnp.where(p_pattern[i, row] > 0, tile, value)
                    out_ref[pl.ds(s * half + a * TILE, TILE), :] = value

    def note(odd):
        for out_ref, m in ((keep_ref, int(odd)), (send_ref, 1 - int(odd))):
            value = jnp.zeros((META, TILE), jnp.float32)
            for a in range(tiles):
                for i in range(width):
                    value = jnp.where(line == a * width + i, p_pattern[i, m * tiles + a].astype(jnp.float32), value)
            out_ref[pl.ds(SLOTS * half, META), :] = value.astype(out_ref.dtype)

    copies[0].wait()
    copies[1].wait()
    for odd in (False, True):
        parity = (r % 2 == 1) == odd

        @pl.when(parity)
        def _(odd=odd):
            note(odd)

        for name in range(len(UNITS)):
            @pl.when(parity & (c == sources[name]))
            def _(name=name, odd=odd):
                pack(name, odd)

    @pl.when(functools.reduce(jnp.logical_and, [c != s for s in sources]))
    def _():
        for out in (keep_ref, send_ref):
            out[pl.ds(0, SLOTS * half), :] = jnp.zeros((SLOTS * half, TILE), p_ref.dtype)

    copies[2].wait()
    copies[3].wait()
    count = ap_ref.shape[0] // TILE
    shift = jnp.where(r % 2 == 1, count // 2, 0)
    for a in range(count):
        row = lax.rem(a + shift, count)
        rows = pl.ds(pl.multiple_of(row * TILE, TILE), TILE)
        for b in range(ap_ref.shape[1] // TILE):
            tile = ap_ref[rows, pl.ds(b * TILE, TILE)]
            out_ref[pl.ds(a * TILE, TILE), pl.ds(b * TILE, TILE)] = jnp.where(ap_pattern[b, row] > 0, tile, zeros)


def merge_kernel(keep_ref, got_ref, half_ref):
    odd = lax.axis_index("row") % 2 == 1
    size = keep_ref.shape[0] - META
    half_ref[pl.ds(0, size), :] = keep_ref[pl.ds(0, size), :] + got_ref[pl.ds(0, size), :]
    mine, theirs = keep_ref[pl.ds(size, META), :], got_ref[pl.ds(size, META), :]
    half_ref[pl.ds(size, META), :] = jnp.where(odd, theirs, mine)
    half_ref[pl.ds(size + META, META), :] = jnp.where(odd, mine, theirs)


def put_columns(out_ref, start, ap):
    rows = ap.shape[0]
    for b in range(ap.shape[1] // TILE):
        out_ref[pl.ds(start + b * rows, rows), :] = ap[:, b * TILE : (b + 1) * TILE]


def far_forward_kernel(cols, own, cross, out_ref):
    c = lax.axis_index("col")
    inner = (cols == 8) & (c >= 2) & (c < 6)

    @pl.when(inner)
    def _():
        out_ref[...] = cross[...]

    @pl.when(jnp.logical_not(inner))
    def _():
        out_ref[...] = own[...]


def diagonal_forward_kernel(pair, cross, out_ref):
    c = lax.axis_index("col")
    by_pair = (c % 2 == 0) == ((c // 2) % 2 == 0)

    @pl.when(by_pair)
    def _():
        out_ref[...] = pair[...]

    @pl.when(jnp.logical_not(by_pair))
    def _():
        out_ref[...] = cross[...]


def swap_kernel(side, pair, cross, own_ap, far_ap, out_ref):
    size = side.shape[0]
    for j, buffer in enumerate((side, pair, cross)):
        out_ref[pl.ds(j * size, size), :] = buffer[...]
    depth = own_ap.shape[0] // 2
    start = len(FIRST) * size
    put_columns(out_ref, start, own_ap[pl.ds(depth, depth), :])
    put_columns(out_ref, start + own_ap.shape[0], far_ap[pl.ds(0, depth), :])


def last_swap_kernel(far, diag, out_ref):
    size = far.shape[0]
    for j, buffer in enumerate((far, diag)):
        out_ref[pl.ds(j * size, size), :] = buffer[...]


def product(p, ap):
    return lax.dot_general(p, ap, (((0,), (0,)), ((), ())), preferred_element_type=jnp.float32)


def accumulate(cols, name, valid, buffers, c_ref, block, read_ap, half, width):
    r, c = lax.axis_index("row"), lax.axis_index("col")
    odd = r % 2 == 1
    data = SLOTS * half
    stride = data + META
    source = class_sources(r, cols)[name]
    at = kind_sources(c, cols)
    inside = valid & (source >= 0) & (source < cols)
    here = [inside & (at[kind] == source) for kind in buffers]
    start = {True: pl.multiple_of(jnp.where(odd, stride, 0), META), False: pl.multiple_of(jnp.where(odd, 0, stride), META)}

    @pl.when(functools.reduce(jnp.logical_or, here))
    def _():
        for flag, (kind, (mine, theirs, row)) in zip(here, buffers.items()):
            @pl.when(flag)
            def _(kind=kind, mine=mine, theirs=theirs, row=row):
                for is_mine, ref, base in ((True, mine, 0), (False, theirs, row)):
                    note = data if kind == OWN else pl.multiple_of(data + jnp.where(odd, META, 0), META)
                    block[pl.ds(start[is_mine], data), :] = ref[pl.ds(base, data), :]
                    block[pl.ds(start[is_mine] + data, META), :] = ref[pl.ds(base + note, META), :]
        for m in sorted({m for m, _ in UNITS[name]}):
            pattern = block[pl.ds(m * stride + data, META), :].astype(jnp.float32)
            ap = read_ap(m)
            for i in [i for mm, i in UNITS[name] if mm == m]:
                slot = jnp.where(odd, slot_of(name, i, True, width), slot_of(name, i, False, width))
                first = pl.multiple_of(m * stride + slot * half, META)
                lhs = []
                for a in range(half // TILE):
                    line = a * width + i
                    weight = jnp.broadcast_to(pattern[line : line + 1, :], (TILE, TILE)).astype(block.dtype)
                    lhs.append(block[pl.ds(first + a * TILE, TILE), :] * weight)
                c_ref[pl.ds(i * TILE, TILE), :] += product(jnp.concatenate(lhs, axis=0), ap)


def readers(odd, half):
    depth = 2 * half

    def in_order(ref, upper):
        row = jnp.where(odd == upper, 0, depth)
        return lambda m: ref[pl.ds(pl.multiple_of(row + m * half, TILE), half), :]

    def columns(ref, start):
        return lambda m: jnp.concatenate([ref[pl.ds(start + b * depth + m * half, half), :] for b in range(2)], axis=1)

    return in_order, columns


def add_all(cols, half, width, buffers, own_ap, far_ap, swapped, size, cross_ap, c_ref, block):
    odd = lax.axis_index("row") % 2 == 1
    in_order, columns = readers(odd, half)
    for name in MAINS:
        accumulate(cols, name, True, buffers, c_ref, block, in_order(own_ap, name == 1), half, width)
    core, cross = columns(swapped, len(FIRST) * size), columns(cross_ap, cross_ap.shape[0] - own_ap.shape[0])
    for name, valid in zip(NEARS, (odd, jnp.logical_not(odd))):
        accumulate(cols, name, valid, buffers, c_ref, block, core, half, width)
        accumulate(cols, name, jnp.logical_not(valid), buffers, c_ref, block, cross, half, width)
    for name in FARS:
        accumulate(cols, name, True, buffers, c_ref, block, in_order(far_ap, name == 5), half, width)


def near_kernel(cols, half, width, own_ap, far_ap, keep, send, side, pair, cross, swapped, cross_ap, c_ref, block):
    size = side.shape[0]
    buffers = {OWN: (keep, send, 0)}
    buffers |= {kind: (ref, swapped, j * size) for j, (kind, ref) in enumerate(zip(FIRST, (side, pair, cross)))}
    c_ref[...] = jnp.zeros_like(c_ref)
    add_all(cols, half, width, buffers, own_ap, far_ap, swapped, size, cross_ap, c_ref, block)


def far_kernel(cols, half, width, own_ap, far_ap, swapped, cross_ap, far, diag, last, partial, c_ref, block):
    size = far.shape[0]
    buffers = {kind: (ref, last, j * size) for j, (kind, ref) in enumerate(zip(SECOND, (far, diag)))}
    c_ref[...] = partial[...]
    add_all(cols, half, width, buffers, own_ap, far_ap, swapped, size, cross_ap, c_ref, block)


def on_device(rows, cols, prolong, applied, prolong_pattern, applied_pattern):
    depth, width = prolong.shape[0], prolong.shape[1] // TILE
    half = depth // 2
    data = SLOTS * half
    size = data + 2 * META
    vmem = pl.BlockSpec(memory_space=pltpu.VMEM)
    smem = pl.BlockSpec(memory_space=pltpu.SMEM)
    params = pltpu.CompilerParams(vmem_limit_bytes=24 << 20)
    shape = lambda *s: jax.ShapeDtypeStruct(s, prolong.dtype)

    def call(kernel, name, out_shape, *operands, specs=None, weight=0, **more):
        if weight:
            more["cost_estimate"] = pl.CostEstimate(flops=weight * 1_000_000_000, bytes_accessed=weight * 3_000_000, transcendentals=0)
        out_specs = (vmem,) * len(out_shape) if isinstance(out_shape, tuple) else vmem
        return pl.pallas_call(
            kernel, out_shape=out_shape, in_specs=specs or [vmem] * len(operands), out_specs=out_specs,
            compiler_params=params, name=name, **more,
        )(*operands)

    def move(x, pairs):
        return lax.ppermute(x, AXES, pairs)

    def row_pairs(pairs):
        return [(a * cols + c, b * cols + c) for a, b in pairs for c in range(cols)]

    def col_pairs(pairs):
        return [(r * cols + a, r * cols + b) for r in range(rows) for a, b in pairs if 0 <= b < cols]

    partner = row_pairs([(r, r ^ 1) for r in range(rows)])
    opposite = [(r, (r + rows // 2) % rows) for r in range(rows)]

    hbm = pl.BlockSpec(memory_space=pltpu.HBM)
    keep, send, own_ap = call(
        functools.partial(prepare_kernel, cols), "prepare", (shape(data + META, TILE),) * 2 + (shape(*applied.shape),),
        *[pltpu.with_memory_space_constraint(x, pltpu.HBM) for x in (prolong, applied, prolong_pattern.T, applied_pattern.T)],
        specs=[hbm] * 4,
        scratch_shapes=[
            pltpu.VMEM(prolong.shape, prolong.dtype),
            pltpu.VMEM(applied.shape, applied.dtype),
            pltpu.SMEM(prolong_pattern.shape[::-1], jnp.int32),
            pltpu.SMEM(applied_pattern.shape[::-1], jnp.int32),
            pltpu.SemaphoreType.DMA((4,)),
        ],
    )
    got = move(send, partner)
    far_ap = move(own_ap, row_pairs(opposite))
    mine = call(merge_kernel, "merge", shape(size, TILE), keep, got)
    middle = lambda c: 2 <= c < cols - 2
    step = lambda c: c - 2 if (c // 2) % 2 == 0 else c + 2
    cross = move(mine, [
        (r * cols + c, r * cols + step(c) if middle(c) else (r ^ 1) * cols + c) for r in range(rows) for c in range(cols)
    ])
    pair = move(mine, col_pairs([(c, c ^ 2) for c in range(cols)]))
    side = move(mine, col_pairs([(c, c ^ 1) for c in range(cols)]))

    ap_rows = 2 * depth
    if cols == 8:
        far_pairs = [(0, 4), (1, 5), (2, 0), (3, 1), (4, 6), (5, 7), (6, 2), (7, 3)]
    else:
        far_pairs = [(c, (c + cols // 2) % cols) for c in range(cols)]
    far_send = call(functools.partial(far_forward_kernel, cols), "far_forward", shape(size, TILE), mine, cross)
    far = move(far_send, col_pairs(far_pairs))
    diag_send = call(diagonal_forward_kernel, "diagonal_forward", shape(size, TILE), pair, cross)
    diag = move(diag_send, col_pairs([(c, c ^ 1) for c in range(cols)]))
    swap = call(swap_kernel, "swap", shape(len(FIRST) * size + 2 * ap_rows, TILE), side, pair, cross, own_ap, far_ap)
    swapped = move(swap, partner)
    last = move(call(last_swap_kernel, "last_swap", shape(len(SECOND) * size, TILE), far, diag, weight=LAST_WEIGHT), partner)
    beyond = [(r, r + 1 if r % 2 == 1 else r - 1) for r in range(rows)]
    relay = [((r + rows // 2) % rows, t) for r, t in beyond if 0 <= t < rows]
    if all(h ^ 1 == t for h, t in relay):
        cross_ap = swapped
    else:
        first = own_ap[:depth].reshape(depth, 2, TILE).transpose(1, 0, 2).reshape(ap_rows, TILE)
        cross_ap = move(first, row_pairs([(r, t) for r, t in beyond if 0 <= t < rows]))

    result = jax.ShapeDtypeStruct((prolong.shape[1], applied.shape[1]), jnp.float32)
    scratch = dict(scratch_shapes=[pltpu.VMEM((2 * (data + META), TILE), prolong.dtype)])
    partial = call(
        functools.partial(near_kernel, cols, half, width), "near", result,
        own_ap, far_ap, keep, send, side, pair, cross, swapped, cross_ap, **scratch,
    )
    return call(
        functools.partial(far_kernel, cols, half, width), "far", result,
        own_ap, far_ap, swapped, cross_ap, far, diag, last, partial, **scratch,
    )


def solution(mesh):
    in_specs = (P("col", "row"), P("row", "col"), P("col", "row"), P("row", "col"))
    return jax.shard_map(
        functools.partial(on_device, mesh.shape["row"], mesh.shape["col"]),
        mesh=mesh, in_specs=in_specs, out_specs=P("row", "col"), check_vma=False,
    )
```

```python
import functools

import jax
import jax.numpy as jnp
from jax import lax
from jax.experimental import pallas as pl
from jax.experimental.pallas import tpu as pltpu
from jax.sharding import PartitionSpec as P

TILE = 128
AXES = ("row", "col")
LAST_WEIGHT, FIRST_WEIGHT = 20, 5
SLOTS = 3
META = 16
MAINS, NEARS, FARS = (0, 1), (2, 3), (4, 5)
UNITS = (
    ((0, 0), (0, 1), (0, 2), (1, 0), (1, 1), (1, 2), (1, 3)),
    ((0, 0), (0, 1), (0, 2), (0, 3), (1, 1), (1, 2), (1, 3)),
    ((0, 0), (1, 0), (1, 1)),
    ((0, 2), (0, 3), (1, 3)),
    ((0, 0), (1, 1)),
    ((0, 2), (1, 3)),
)
OWN, SIDE, PAIR, CROSS, FAR, DIAG = range(6)
FIRST, SECOND = (OWN, SIDE, PAIR, CROSS), (FAR, DIAG)


def class_sources(r, cols):
    rem = lambda x: lax.rem(x, cols)
    return (2 * r, 2 * r + 1, 2 * r - 1, 2 * r + 2, rem(2 * r + cols // 2), rem(2 * r + 1 + cols // 2))


def kind_sources(c, cols):
    even, low = c % 2 == 0, (c // 2) % 2 == 0
    near, past = jnp.where(even, c + 1, c - 1), jnp.where(even, c - 1, c + 1)
    pair, across = jnp.where(low, c + 2, c - 2), jnp.where(low, c - 2, c + 2)
    return {OWN: c, SIDE: near, PAIR: pair, CROSS: across, FAR: lax.rem(c + cols // 2, cols), DIAG: past}


def slot_of(name, i, odd, width):
    return 2 if name in FARS else (i + (width if odd else 0)) % SLOTS


def prepare_kernel(cols, p_hbm, ap_hbm, p_pattern_hbm, ap_pattern_hbm, keep_ref, send_ref, first_ref, second_ref, p_ref, ap_ref, p_pattern, ap_pattern, sems):
    copies = [
        pltpu.make_async_copy(source, target, sems.at[i])
        for i, (source, target) in enumerate(
            ((p_pattern_hbm, p_pattern), (p_hbm, p_ref), (ap_pattern_hbm, ap_pattern), (ap_hbm, ap_ref))
        )
    ]
    for copy in copies:
        copy.start()
    r, c = lax.axis_index("row"), lax.axis_index("col")
    tiles = p_ref.shape[0] // TILE // 2
    half = tiles * TILE
    width = p_ref.shape[1] // TILE
    sources = class_sources(r, cols)
    zeros = jnp.zeros((TILE, TILE), p_ref.dtype)
    line = lax.broadcasted_iota(jnp.int32, (META, TILE), 0)

    def pack(name, odd):
        for out_ref, m in ((keep_ref, int(odd)), (send_ref, 1 - int(odd))):
            for s in range(SLOTS):
                found = [i for mm, i in UNITS[name] if mm == m and slot_of(name, i, odd, width) == s]
                for a in range(tiles):
                    value, row = zeros, m * tiles + a
                    for i in found:
                        tile = p_ref[pl.ds(row * TILE, TILE), pl.ds(i * TILE, TILE)]
                        value = jnp.where(p_pattern[i, row] > 0, tile, value)
                    out_ref[pl.ds(s * half + a * TILE, TILE), :] = value

    def note(odd):
        for out_ref, m in ((keep_ref, int(odd)), (send_ref, 1 - int(odd))):
            value = jnp.zeros((META, TILE), jnp.float32)
            for a in range(tiles):
                for i in range(width):
                    value = jnp.where(line == a * width + i, p_pattern[i, m * tiles + a].astype(jnp.float32), value)
            out_ref[pl.ds(SLOTS * half, META), :] = value.astype(out_ref.dtype)

    copies[0].wait()
    copies[1].wait()
    for odd in (False, True):
        parity = (r % 2 == 1) == odd

        @pl.when(parity)
        def _(odd=odd):
            note(odd)

        for name in range(len(UNITS)):
            @pl.when(parity & (c == sources[name]))
            def _(name=name, odd=odd):
                pack(name, odd)

    @pl.when(functools.reduce(jnp.logical_and, [c != s for s in sources]))
    def _():
        for out in (keep_ref, send_ref):
            out[pl.ds(0, SLOTS * half), :] = jnp.zeros((SLOTS * half, TILE), p_ref.dtype)

    copies[2].wait()
    copies[3].wait()
    count = ap_ref.shape[0] // TILE
    shift = jnp.where(r % 2 == 1, count // 2, 0)
    for a in range(count):
        row = lax.rem(a + shift, count)
        rows = pl.ds(pl.multiple_of(row * TILE, TILE), TILE)
        for b in range(ap_ref.shape[1] // TILE):
            tile = ap_ref[rows, pl.ds(b * TILE, TILE)]
            out_ref = first_ref if 2 * a < count else second_ref
            out_ref[pl.ds(a % (count // 2) * TILE, TILE), pl.ds(b * TILE, TILE)] = jnp.where(ap_pattern[b, row] > 0, tile, zeros)


def merge_kernel(keep_ref, got_ref, half_ref):
    odd = lax.axis_index("row") % 2 == 1
    size = keep_ref.shape[0] - META
    half_ref[pl.ds(0, size), :] = keep_ref[pl.ds(0, size), :] + got_ref[pl.ds(0, size), :]
    mine, theirs = keep_ref[pl.ds(size, META), :], got_ref[pl.ds(size, META), :]
    half_ref[pl.ds(size, META), :] = jnp.where(odd, theirs, mine)
    half_ref[pl.ds(size + META, META), :] = jnp.where(odd, mine, theirs)


def far_forward_kernel(cols, own, cross, ordered_after, out_ref):
    c = lax.axis_index("col")
    inner = (cols == 8) & (c >= 2) & (c < 6)

    @pl.when(inner)
    def _():
        out_ref[...] = cross[...]

    @pl.when(jnp.logical_not(inner))
    def _():
        out_ref[...] = own[...]


def diagonal_forward_kernel(pair, cross, ordered_after, out_ref):
    c = lax.axis_index("col")
    by_pair = (c % 2 == 0) == ((c // 2) % 2 == 0)

    @pl.when(by_pair)
    def _():
        out_ref[...] = pair[...]

    @pl.when(jnp.logical_not(by_pair))
    def _():
        out_ref[...] = cross[...]


def swap_kernel(own, side, pair, cross, own_second, far_first, out_ref):
    size = side.shape[0]
    for j, buffer in enumerate((own, side, pair, cross)):
        for a in range(0, size - 2 * META, TILE):
            out_ref[pl.ds(j * size + a, TILE), :] = buffer[pl.ds(a, TILE), :].T
        out_ref[pl.ds((j + 1) * size - 2 * META, 2 * META), :] = buffer[pl.ds(size - 2 * META, 2 * META), :]
    start = len(FIRST) * size
    for ap in (own_second, far_first):
        for b in range(ap.shape[1] // TILE):
            out_ref[pl.ds(start, ap.shape[0]), :] = ap[:, b * TILE : (b + 1) * TILE]
            start += ap.shape[0]


def settle_kernel(ap_ref, ordered_after, out_ref):
    out_ref[...] = ap_ref[...]


def last_swap_kernel(far, diag, ordered_after, out_ref):
    size = far.shape[0]
    for j, buffer in enumerate((far, diag)):
        out_ref[pl.ds(j * size, size), :] = buffer[...]


def add_product(c_ref, ref, base, name, m, odd, half, width, ap, transposed):
    note = base + SLOTS * half + (META if odd else 0)
    pattern = ref[pl.ds(pl.multiple_of(note, META), META), :].astype(jnp.float32)
    found = [i for mm, i in UNITS[name] if mm == m]
    columns = []
    for i in found:
        tiles = []
        for a in range(half // TILE):
            k = a * width + i
            weight = jnp.broadcast_to(pattern[k : k + 1, :], (TILE, TILE)).astype(ref.dtype)
            first = base + slot_of(name, i, odd, width) * half + a * TILE
            tiles.append(ref[pl.ds(pl.multiple_of(first, META), TILE), :] * weight)
        columns.append(jnp.concatenate(tiles, axis=int(transposed)))
    lhs = jnp.concatenate(columns, axis=1 - int(transposed))
    product = lax.dot_general(lhs, ap, (((int(transposed),), (0,)), ((), ())), preferred_element_type=jnp.float32)
    c_ref[pl.ds(found[0] * TILE, len(found) * TILE), :] += product


def present(cols, name, kind, valid=True):
    r, c = lax.axis_index("row"), lax.axis_index("col")
    source = class_sources(r, cols)[name]
    return valid & (source >= 0) & (source < cols) & (kind_sources(c, cols)[kind] == source)


def read_applied(name, m, odd, half, size, own, far, swapped, cross_ap):
    depth, rows = 2 * half, pl.ds(m * half, half)
    if name in MAINS:
        return own[int(odd == (name == 0))][rows, :]
    if name in FARS:
        return far[int(odd == (name == 4))][rows, :]
    if odd == (name == 2):
        ref, start = swapped, len(FIRST) * size
    else:
        ref, start = cross_ap, cross_ap.shape[0] - 2 * depth
    return jnp.concatenate([ref[pl.ds(start + b * depth + m * half, half), :] for b in range(2)], axis=1)


def add_blocks(cols, half, width, c_ref, read, kinds, size, mine, theirs, transposed):
    row_odd = lax.axis_index("row") % 2 == 1
    for odd in (False, True):
        @pl.when(row_odd == odd)
        def _(odd=odd):
            for name in range(len(UNITS)):
                here = [present(cols, name, kind) for kind in kinds]
                base = sum(jnp.where(flag, j * size, 0) for j, flag in enumerate(here))

                @pl.when(functools.reduce(jnp.logical_or, here))
                def _(name=name, base=base):
                    for m in sorted({m for m, _ in UNITS[name]}):
                        ref = mine if odd == (m == 1) else theirs
                        if ref is not None:
                            add_product(c_ref, ref, base, name, m, odd, half, width, read(name, m, odd), transposed)


def near_kernel(cols, half, width, own_first, own_second, far_first, far_second, swapped, cross_ap, swap, last_swap, c_ref):
    size = last_swap.shape[0] // len(SECOND)
    read = lambda name, m, odd: read_applied(
        name, m, odd, half, size, (own_first, own_second), (far_first, far_second), swapped, cross_ap
    )
    c_ref[...] = jnp.zeros_like(c_ref)
    add_blocks(cols, half, width, c_ref, read, FIRST, size, swap, swapped, True)
    add_blocks(cols, half, width, c_ref, read, SECOND, size, last_swap, None, False)


def last_kernel(cols, half, width, own_first, own_second, far_first, far_second, swapped, cross_ap, last, partial, c_ref):
    size = last.shape[0] // len(SECOND)
    read = lambda name, m, odd: read_applied(
        name, m, odd, half, size, (own_first, own_second), (far_first, far_second), swapped, cross_ap
    )
    c_ref[...] = partial[...]
    add_blocks(cols, half, width, c_ref, read, SECOND, size, None, last, False)


def on_device(rows, cols, prolong, applied, prolong_pattern, applied_pattern):
    depth, width = prolong.shape[0], prolong.shape[1] // TILE
    half = depth // 2
    data = SLOTS * half
    size = data + 2 * META
    vmem = pl.BlockSpec(memory_space=pltpu.VMEM)
    smem = pl.BlockSpec(memory_space=pltpu.SMEM)
    params = pltpu.CompilerParams(vmem_limit_bytes=24 << 20)
    shape = lambda *s: jax.ShapeDtypeStruct(s, prolong.dtype)

    def call(kernel, name, out_shape, *operands, specs=None, weight=0, **more):
        if weight:
            more["cost_estimate"] = pl.CostEstimate(flops=weight * 1_000_000_000, bytes_accessed=weight * 3_000_000, transcendentals=0)
        out_specs = (vmem,) * len(out_shape) if isinstance(out_shape, tuple) else vmem
        return pl.pallas_call(
            kernel, out_shape=out_shape, in_specs=specs or [vmem] * len(operands), out_specs=out_specs,
            compiler_params=params, name=name, **more,
        )(*operands)

    def move(x, pairs):
        return lax.ppermute(x, AXES, pairs)

    def row_pairs(pairs):
        return [(a * cols + c, b * cols + c) for a, b in pairs for c in range(cols)]

    def col_pairs(pairs):
        return [(r * cols + a, r * cols + b) for r in range(rows) for a, b in pairs if 0 <= b < cols]

    partner = row_pairs([(r, r ^ 1) for r in range(rows)])
    opposite = [(r, (r + rows // 2) % rows) for r in range(rows)]

    hbm = pl.BlockSpec(memory_space=pltpu.HBM)
    half_ap = shape(depth, applied.shape[1])
    keep, send, own_first, own_second = call(
        functools.partial(prepare_kernel, cols), "prepare", (shape(data + META, TILE),) * 2 + (half_ap,) * 2,
        *[pltpu.with_memory_space_constraint(x, pltpu.HBM) for x in (prolong, applied, prolong_pattern.T, applied_pattern.T)],
        specs=[hbm] * 4,
        scratch_shapes=[
            pltpu.VMEM(prolong.shape, prolong.dtype),
            pltpu.VMEM(applied.shape, applied.dtype),
            pltpu.SMEM(prolong_pattern.shape[::-1], jnp.int32),
            pltpu.SMEM(applied_pattern.shape[::-1], jnp.int32),
            pltpu.SemaphoreType.DMA((4,)),
        ],
    )
    got = move(send, partner)
    far_first, far_second = move(own_first, row_pairs(opposite)), move(own_second, row_pairs(opposite))
    mine = call(merge_kernel, "merge", shape(size, TILE), keep, got)
    middle = lambda c: 2 <= c < cols - 2
    step = lambda c: c - 2 if (c // 2) % 2 == 0 else c + 2
    cross = move(mine, [
        (r * cols + c, r * cols + step(c) if middle(c) else (r ^ 1) * cols + c) for r in range(rows) for c in range(cols)
    ])
    pair = move(mine, col_pairs([(c, c ^ 2) for c in range(cols)]))
    side = move(mine, col_pairs([(c, c ^ 1) for c in range(cols)]))

    if cols == 8:
        far_pairs = [(0, 4), (1, 5), (2, 0), (3, 1), (4, 6), (5, 7), (6, 2), (7, 3)]
    else:
        far_pairs = [(c, (c + cols // 2) % cols) for c in range(cols)]
    diag_send = call(diagonal_forward_kernel, "diagonal_forward", shape(size, TILE), pair, cross, pair)
    diag = move(diag_send, col_pairs([(c, c ^ 1) for c in range(cols)]))
    far_send = call(
        functools.partial(far_forward_kernel, cols), "far_forward", shape(size, TILE), mine, cross, cross
    )
    far = move(far_send, col_pairs(far_pairs))
    far_first = call(settle_kernel, "settle_first", half_ap, far_first, mine, weight=FIRST_WEIGHT)
    swap = call(
        swap_kernel, "swap", shape(len(FIRST) * size + 4 * depth, TILE), mine, side, pair, cross, own_second, far_first
    )
    swapped = move(swap, partner)
    far_second = call(settle_kernel, "settle", half_ap, far_second, swap)
    last_swap = call(last_swap_kernel, "last_swap", shape(len(SECOND) * size, TILE), far, diag, far_second, weight=LAST_WEIGHT)
    last = move(last_swap, partner)
    beyond = [(r, r + 1 if r % 2 == 1 else r - 1) for r in range(rows)]
    relay = [((r + rows // 2) % rows, t) for r, t in beyond if 0 <= t < rows]
    if all(h ^ 1 == t for h, t in relay):
        cross_ap = swapped
    else:
        first = own_first.reshape(depth, 2, TILE).transpose(1, 0, 2).reshape(2 * depth, TILE)
        cross_ap = move(first, row_pairs([(r, t) for r, t in beyond if 0 <= t < rows]))

    result = jax.ShapeDtypeStruct((prolong.shape[1], applied.shape[1]), jnp.float32)
    sizes = (cols, half, width)
    aps = (own_first, own_second, far_first, far_second, swapped, cross_ap)
    partial = call(
        functools.partial(near_kernel, *sizes), "near", result, *aps, swap, last_swap,
    )
    return call(functools.partial(last_kernel, *sizes), "last", result, *aps, last, partial)


def solution(mesh):
    in_specs = (P("col", "row"), P("row", "col"), P("col", "row"), P("row", "col"))
    return jax.shard_map(
        functools.partial(on_device, mesh.shape["row"], mesh.shape["col"]),
        mesh=mesh, in_specs=in_specs, out_specs=P("row", "col"), check_vma=False,
    )
```

```python
import functools

import jax
import jax.numpy as jnp
from jax import lax
from jax.experimental import pallas as pl
from jax.experimental.pallas import tpu as pltpu
from jax.sharding import PartitionSpec as P

TILE = 128
AXES = ("row", "col")
LAST_WEIGHT, FIRST_WEIGHT = 20, 5
SLOTS = 3
META = 16
MAINS, NEARS, FARS = (0, 1), (2, 3), (4, 5)
UNITS = (
    ((0, 0), (0, 1), (0, 2), (1, 0), (1, 1), (1, 2), (1, 3)),
    ((0, 0), (0, 1), (0, 2), (0, 3), (1, 1), (1, 2), (1, 3)),
    ((0, 0), (1, 0), (1, 1)),
    ((0, 2), (0, 3), (1, 3)),
    ((0, 0), (1, 1)),
    ((0, 2), (1, 3)),
)
OWN, SIDE, PAIR, CROSS, FAR, DIAG = range(6)
FIRST, SECOND = (OWN, SIDE, PAIR, CROSS), (FAR, DIAG)


def class_sources(r, cols):
    rem = lambda x: lax.rem(x, cols)
    return (2 * r, 2 * r + 1, 2 * r - 1, 2 * r + 2, rem(2 * r + cols // 2), rem(2 * r + 1 + cols // 2))


def kind_sources(c, cols):
    even, low = c % 2 == 0, (c // 2) % 2 == 0
    near, past = jnp.where(even, c + 1, c - 1), jnp.where(even, c - 1, c + 1)
    pair, across = jnp.where(low, c + 2, c - 2), jnp.where(low, c - 2, c + 2)
    return {OWN: c, SIDE: near, PAIR: pair, CROSS: across, FAR: lax.rem(c + cols // 2, cols), DIAG: past}


def slot_of(name, i, odd, width):
    return 2 if name in FARS else (i + (width if odd else 0)) % SLOTS


def prepare_kernel(cols, p_hbm, ap_hbm, p_pattern_hbm, ap_pattern_hbm, keep_ref, send_ref, first_ref, second_ref, p_ref, ap_ref, p_pattern, ap_pattern, sems):
    copies = [
        pltpu.make_async_copy(source, target, sems.at[i])
        for i, (source, target) in enumerate(
            ((p_pattern_hbm, p_pattern), (p_hbm, p_ref), (ap_pattern_hbm, ap_pattern), (ap_hbm, ap_ref))
        )
    ]
    for copy in copies:
        copy.start()
    r, c = lax.axis_index("row"), lax.axis_index("col")
    tiles = p_ref.shape[0] // TILE // 2
    half = tiles * TILE
    width = p_ref.shape[1] // TILE
    sources = class_sources(r, cols)
    zeros = jnp.zeros((TILE, TILE), p_ref.dtype)
    line = lax.broadcasted_iota(jnp.int32, (META, TILE), 0)

    def pack(name, odd):
        for out_ref, m in ((keep_ref, int(odd)), (send_ref, 1 - int(odd))):
            for s in range(SLOTS):
                found = [i for mm, i in UNITS[name] if mm == m and slot_of(name, i, odd, width) == s]
                for a in range(tiles):
                    value, row = zeros, m * tiles + a
                    for i in found:
                        tile = p_ref[pl.ds(row * TILE, TILE), pl.ds(i * TILE, TILE)]
                        value = jnp.where(p_pattern[i, row] > 0, tile, value)
                    out_ref[pl.ds(s * half + a * TILE, TILE), :] = value

    def note(odd):
        for out_ref, m in ((keep_ref, int(odd)), (send_ref, 1 - int(odd))):
            value = jnp.zeros((META, TILE), jnp.float32)
            for a in range(tiles):
                for i in range(width):
                    value = jnp.where(line == a * width + i, p_pattern[i, m * tiles + a].astype(jnp.float32), value)
            out_ref[pl.ds(SLOTS * half, META), :] = value.astype(out_ref.dtype)

    copies[0].wait()
    copies[1].wait()
    for odd in (False, True):
        parity = (r % 2 == 1) == odd

        @pl.when(parity)
        def _(odd=odd):
            note(odd)

        for name in range(len(UNITS)):
            @pl.when(parity & (c == sources[name]))
            def _(name=name, odd=odd):
                pack(name, odd)

    @pl.when(functools.reduce(jnp.logical_and, [c != s for s in sources]))
    def _():
        for out in (keep_ref, send_ref):
            out[pl.ds(0, SLOTS * half), :] = jnp.zeros((SLOTS * half, TILE), p_ref.dtype)

    copies[2].wait()
    copies[3].wait()
    count = ap_ref.shape[0] // TILE
    shift = jnp.where(r % 2 == 1, count // 2, 0)
    for a in range(count):
        row = lax.rem(a + shift, count)
        rows = pl.ds(pl.multiple_of(row * TILE, TILE), TILE)
        for b in range(ap_ref.shape[1] // TILE):
            tile = ap_ref[rows, pl.ds(b * TILE, TILE)]
            out_ref = first_ref if 2 * a < count else second_ref
            out_ref[pl.ds(a % (count // 2) * TILE, TILE), pl.ds(b * TILE, TILE)] = jnp.where(ap_pattern[b, row] > 0, tile, zeros)


def merge_kernel(keep_ref, got_ref, half_ref):
    odd = lax.axis_index("row") % 2 == 1
    size = keep_ref.shape[0] - META
    half_ref[pl.ds(0, size), :] = keep_ref[pl.ds(0, size), :] + got_ref[pl.ds(0, size), :]
    mine, theirs = keep_ref[pl.ds(size, META), :], got_ref[pl.ds(size, META), :]
    half_ref[pl.ds(size, META), :] = jnp.where(odd, theirs, mine)
    half_ref[pl.ds(size + META, META), :] = jnp.where(odd, mine, theirs)


def far_forward_kernel(cols, own, cross, ordered_after, out_ref):
    c = lax.axis_index("col")
    inner = (cols == 8) & (c >= 2) & (c < 6)

    @pl.when(inner)
    def _():
        out_ref[...] = cross[...]

    @pl.when(jnp.logical_not(inner))
    def _():
        out_ref[...] = own[...]


def diagonal_forward_kernel(pair, cross, ordered_after, out_ref):
    c = lax.axis_index("col")
    by_pair = (c % 2 == 0) == ((c // 2) % 2 == 0)

    @pl.when(by_pair)
    def _():
        out_ref[...] = pair[...]

    @pl.when(jnp.logical_not(by_pair))
    def _():
        out_ref[...] = cross[...]


def swap_kernel(own, side, pair, cross, own_second, far_first, out_ref):
    size = side.shape[0]
    for j, buffer in enumerate((own, side, pair, cross)):
        for a in range(0, size - 2 * META, TILE):
            out_ref[pl.ds(j * size + a, TILE), :] = buffer[pl.ds(a, TILE), :].T
        out_ref[pl.ds((j + 1) * size - 2 * META, 2 * META), :] = buffer[pl.ds(size - 2 * META, 2 * META), :]
    start = len(FIRST) * size
    for ap in (own_second, far_first):
        for b in range(ap.shape[1] // TILE):
            out_ref[pl.ds(start, ap.shape[0]), :] = ap[:, b * TILE : (b + 1) * TILE]
            start += ap.shape[0]


def pass_kernel(ref, ordered_after, out_ref):
    out_ref[...] = ref[...]


def masked_product(ref, base, flag, odd, slots, half, width, ap, transposed):
    note = base + SLOTS * half + (META if odd else 0)
    pattern = ref[pl.ds(pl.multiple_of(note, META), META), :].astype(jnp.float32)
    pattern = pattern * jnp.where(flag, 1.0, 0.0)
    columns = []
    for i, slot in slots.items():
        tiles = []
        for a in range(half // TILE):
            k = a * width + i
            weight = jnp.broadcast_to(pattern[k : k + 1, :], (TILE, TILE)).astype(ref.dtype)
            tiles.append(ref[pl.ds(pl.multiple_of(base + slot + a * TILE, META), TILE), :] * weight)
        columns.append(jnp.concatenate(tiles, axis=int(transposed)))
    lhs = jnp.concatenate(columns, axis=1 - int(transposed))
    product = lax.dot_general(lhs, ap, (((int(transposed),), (0,)), ((), ())), preferred_element_type=jnp.float32)
    return pl.ds(min(slots) * TILE, len(slots) * TILE), product


def present(cols, name, kind, valid=True):
    r, c = lax.axis_index("row"), lax.axis_index("col")
    source = class_sources(r, cols)[name]
    return valid & (source >= 0) & (source < cols) & (kind_sources(c, cols)[kind] == source)


def read_applied(name, m, odd, half, size, own, far, swapped, cross_ap):
    depth, rows = 2 * half, pl.ds(m * half, half)
    if name in MAINS:
        return own[int(odd == (name == 0))][rows, :]
    if name in FARS:
        return far[int(odd == (name == 4))][rows, :]
    if odd == (name == 2):
        ref, start = swapped, len(FIRST) * size
    else:
        ref, start = cross_ap, cross_ap.shape[0] - 2 * depth
    return jnp.concatenate([ref[pl.ds(start + b * depth + m * half, half), :] for b in range(2)], axis=1)


def add_classes(cols, half, width, odd, c_ref, read, kinds, size, mine, theirs, names):
    for name in names:
        here = [present(cols, name, kind) for kind in kinds]
        base = sum(jnp.where(flag, j * size, 0) for j, flag in enumerate(here))
        there = functools.reduce(jnp.logical_or, here)
        for m in sorted({m for m, _ in UNITS[name]}):
            ref = mine if odd == (m == 1) else theirs
            if ref is not None:
                slots = {i: slot_of(name, i, odd, width) * half for mm, i in UNITS[name] if mm == m}
                rows, product = masked_product(ref, base, there, odd, slots, half, width, read(name, m, odd), True)
                c_ref[rows, :] += product


def kind_product(cols, half, width, odd, read, kind, ref, m):
    here = [present(cols, name, kind) for name in range(len(UNITS))]
    there = functools.reduce(jnp.logical_or, here)
    is_far = functools.reduce(jnp.logical_or, [here[name] for name in FARS])
    ap = read(0, m, odd)
    for name in range(1, len(UNITS)):
        ap = jnp.where(here[name], read(name, m, odd), ap)
    slots = {
        i: jnp.where(is_far, slot_of(FARS[0], i, odd, width), slot_of(MAINS[0], i, odd, width)) * half for i in range(width)
    }
    return masked_product(ref, 0, there, odd, slots, half, width, ap, False)[1]


def by_parity(body):
    row_odd = lax.axis_index("row") % 2 == 1
    for odd in (False, True):
        @pl.when(row_odd == odd)
        def _(odd=odd):
            body(odd)


def own_kernel(cols, half, width, own_first, own_second, swap, side, c_ref):
    size = side.shape[0]
    read = lambda name, m, odd: read_applied(name, m, odd, half, size, (own_first, own_second), None, None, None)

    def body(odd):
        c_ref[...] = jnp.zeros_like(c_ref)
        add_classes(cols, half, width, odd, c_ref, read, FIRST, size, swap, None, MAINS)

    by_parity(body)


def near_kernel(cols, half, width, own_first, own_second, far_first, far_second, swapped, cross_ap, swap, diag, far, partial, c_ref):
    size = far.shape[0]
    read = lambda name, m, odd: read_applied(
        name, m, odd, half, size, (own_first, own_second), (far_first, far_second), swapped, cross_ap
    )

    def body(odd):
        mine = int(odd)
        c_ref[...] = partial[...]
        add_classes(cols, half, width, odd, c_ref, read, FIRST, size, None, swapped, MAINS)
        add_classes(cols, half, width, odd, c_ref, read, FIRST, size, swap, swapped, NEARS + FARS)
        c_ref[...] += kind_product(cols, half, width, odd, read, DIAG, diag, mine)
        c_ref[...] += kind_product(cols, half, width, odd, read, FAR, far, mine)

    by_parity(body)


def diagonal_kernel(cols, half, width, own_first, own_second, far_first, far_second, swapped, cross_ap, diag_last, partial, c_ref):
    size = diag_last.shape[0]
    read = lambda name, m, odd: read_applied(
        name, m, odd, half, size, (own_first, own_second), (far_first, far_second), swapped, cross_ap
    )

    def body(odd):
        c_ref[...] = partial[...] + kind_product(cols, half, width, odd, read, DIAG, diag_last, 1 - int(odd))

    by_parity(body)


def last_kernel(cols, half, width, own_first, own_second, far_first, far_second, swapped, cross_ap, far_last, partial, out_hbm, c_ref, sems):
    size = far_last.shape[0]
    read = lambda name, m, odd: read_applied(
        name, m, odd, half, size, (own_first, own_second), (far_first, far_second), swapped, cross_ap
    )

    def body(odd):
        product = kind_product(cols, half, width, odd, read, FAR, far_last, 1 - int(odd))
        copies = []
        for i in range(width):
            rows = pl.ds(i * TILE, TILE)
            c_ref[rows, :] = partial[rows, :] + product[i * TILE : (i + 1) * TILE, :]
            copies.append(pltpu.make_async_copy(c_ref.at[rows, :], out_hbm.at[rows, :], sems.at[i]))
            copies[-1].start()
        for copy in copies:
            copy.wait()

    by_parity(body)


def on_device(rows, cols, prolong, applied, prolong_pattern, applied_pattern):
    depth, width = prolong.shape[0], prolong.shape[1] // TILE
    half = depth // 2
    data = SLOTS * half
    size = data + 2 * META
    vmem = pl.BlockSpec(memory_space=pltpu.VMEM)
    smem = pl.BlockSpec(memory_space=pltpu.SMEM)
    params = pltpu.CompilerParams(vmem_limit_bytes=24 << 20)
    shape = lambda *s: jax.ShapeDtypeStruct(s, prolong.dtype)

    def call(kernel, name, out_shape, *operands, specs=None, weight=0, **more):
        if weight:
            more["cost_estimate"] = pl.CostEstimate(flops=weight * 1_000_000_000, bytes_accessed=weight * 3_000_000, transcendentals=0)
        out_specs = (vmem,) * len(out_shape) if isinstance(out_shape, tuple) else vmem
        return pl.pallas_call(
            kernel, out_shape=out_shape, in_specs=specs or [vmem] * len(operands), out_specs=out_specs,
            compiler_params=params, name=name, **more,
        )(*operands)

    def move(x, pairs):
        return lax.ppermute(x, AXES, pairs)

    def row_pairs(pairs):
        return [(a * cols + c, b * cols + c) for a, b in pairs for c in range(cols)]

    def col_pairs(pairs):
        return [(r * cols + a, r * cols + b) for r in range(rows) for a, b in pairs if 0 <= b < cols]

    partner = row_pairs([(r, r ^ 1) for r in range(rows)])
    opposite = [(r, (r + rows // 2) % rows) for r in range(rows)]

    hbm = pl.BlockSpec(memory_space=pltpu.HBM)
    half_ap = shape(depth, applied.shape[1])
    keep, send, own_first, own_second = call(
        functools.partial(prepare_kernel, cols), "prepare", (shape(data + META, TILE),) * 2 + (half_ap,) * 2,
        *[pltpu.with_memory_space_constraint(x, pltpu.HBM) for x in (prolong, applied, prolong_pattern.T, applied_pattern.T)],
        specs=[hbm] * 4,
        scratch_shapes=[
            pltpu.VMEM(prolong.shape, prolong.dtype),
            pltpu.VMEM(applied.shape, applied.dtype),
            pltpu.SMEM(prolong_pattern.shape[::-1], jnp.int32),
            pltpu.SMEM(applied_pattern.shape[::-1], jnp.int32),
            pltpu.SemaphoreType.DMA((4,)),
        ],
    )
    got = move(send, partner)
    far_first, far_second = move(own_first, row_pairs(opposite)), move(own_second, row_pairs(opposite))
    mine = call(merge_kernel, "merge", shape(size, TILE), keep, got)
    middle = lambda c: 2 <= c < cols - 2
    step = lambda c: c - 2 if (c // 2) % 2 == 0 else c + 2
    cross = move(mine, [
        (r * cols + c, r * cols + step(c) if middle(c) else (r ^ 1) * cols + c) for r in range(rows) for c in range(cols)
    ])
    pair = move(mine, col_pairs([(c, c ^ 2) for c in range(cols)]))
    side = move(mine, col_pairs([(c, c ^ 1) for c in range(cols)]))

    if cols == 8:
        far_pairs = [(0, 4), (1, 5), (2, 0), (3, 1), (4, 6), (5, 7), (6, 2), (7, 3)]
    else:
        far_pairs = [(c, (c + cols // 2) % cols) for c in range(cols)]
    diag_send = call(diagonal_forward_kernel, "diagonal_forward", shape(size, TILE), pair, cross, pair)
    diag = move(diag_send, col_pairs([(c, c ^ 1) for c in range(cols)]))
    far_send = call(
        functools.partial(far_forward_kernel, cols), "far_forward", shape(size, TILE), mine, cross, cross
    )
    far = move(far_send, col_pairs(far_pairs))
    far_first = call(pass_kernel, "settle_first", half_ap, far_first, mine, weight=FIRST_WEIGHT)
    swap = call(
        swap_kernel, "swap", shape(len(FIRST) * size + 4 * depth, TILE), mine, side, pair, cross, own_second, far_first
    )
    swapped = move(swap, partner)
    result = jax.ShapeDtypeStruct((prolong.shape[1], applied.shape[1]), jnp.float32)
    sizes = (cols, half, width)
    partial = call(functools.partial(own_kernel, *sizes), "own", result, own_first, own_second, swap, side)
    far_second = call(pass_kernel, "settle", half_ap, far_second, partial)
    diag_last = move(call(pass_kernel, "pass_diagonal", shape(size, TILE), diag, diag_send), partner)
    far_last = move(call(pass_kernel, "pass_far", shape(size, TILE), far, far_second, weight=LAST_WEIGHT), partner)
    beyond = [(r, r + 1 if r % 2 == 1 else r - 1) for r in range(rows)]
    relay = [((r + rows // 2) % rows, t) for r, t in beyond if 0 <= t < rows]
    if all(h ^ 1 == t for h, t in relay):
        cross_ap = swapped
    else:
        first = own_first.reshape(depth, 2, TILE).transpose(1, 0, 2).reshape(2 * depth, TILE)
        cross_ap = move(first, row_pairs([(r, t) for r, t in beyond if 0 <= t < rows]))

    aps = (own_first, own_second, far_first, far_second, swapped, cross_ap)
    partial = call(functools.partial(near_kernel, *sizes), "near", result, *aps, swap, diag, far, partial)
    partial = call(functools.partial(diagonal_kernel, *sizes), "diagonal", result, *aps, diag_last, partial)
    operands = (*aps, far_last, partial)
    return pl.pallas_call(
        functools.partial(last_kernel, *sizes), out_shape=result, in_specs=[vmem] * len(operands), out_specs=hbm,
        compiler_params=params, name="last",
        scratch_shapes=[pltpu.VMEM(result.shape, jnp.float32), pltpu.SemaphoreType.DMA((width,))],
    )(*operands)


def solution(mesh):
    in_specs = (P("col", "row"), P("row", "col"), P("col", "row"), P("row", "col"))
    return jax.shard_map(
        functools.partial(on_device, mesh.shape["row"], mesh.shape["col"]),
        mesh=mesh, in_specs=in_specs, out_specs=P("row", "col"), check_vma=False,
    )
```

```python
import functools

import jax
import jax.numpy as jnp
from jax import lax
from jax.experimental import pallas as pl
from jax.experimental.pallas import tpu as pltpu
from jax.sharding import PartitionSpec as P

TILE = 128
AXES = ("row", "col")
LAST_WEIGHT, FIRST_WEIGHT = 20, 5
SLOTS = 3
META = 16
MAINS, NEARS, FARS = (0, 1), (2, 3), (4, 5)
UNITS = (
    ((0, 0), (0, 1), (0, 2), (1, 0), (1, 1), (1, 2), (1, 3)),
    ((0, 0), (0, 1), (0, 2), (0, 3), (1, 1), (1, 2), (1, 3)),
    ((0, 0), (1, 0), (1, 1)),
    ((0, 2), (0, 3), (1, 3)),
    ((0, 0), (1, 1)),
    ((0, 2), (1, 3)),
)
OWN, SIDE, PAIR, CROSS, FAR, DIAG = range(6)
FIRST, SECOND = (OWN, SIDE, PAIR, CROSS), (FAR, DIAG)


def class_sources(r, cols):
    rem = lambda x: lax.rem(x, cols)
    return (2 * r, 2 * r + 1, 2 * r - 1, 2 * r + 2, rem(2 * r + cols // 2), rem(2 * r + 1 + cols // 2))


def kind_sources(c, cols):
    even, low = c % 2 == 0, (c // 2) % 2 == 0
    near, past = jnp.where(even, c + 1, c - 1), jnp.where(even, c - 1, c + 1)
    pair, across = jnp.where(low, c + 2, c - 2), jnp.where(low, c - 2, c + 2)
    return {OWN: c, SIDE: near, PAIR: pair, CROSS: across, FAR: lax.rem(c + cols // 2, cols), DIAG: past}


def slot_of(name, i, odd, width):
    return 2 if name in FARS else (i + (width if odd else 0)) % SLOTS


def prepare_kernel(cols, p_hbm, ap_hbm, p_pattern_hbm, ap_pattern_hbm, keep_ref, send_ref, first_ref, second_ref, p_ref, p_pattern, ap_pattern, sems):
    depth = p_ref.shape[0]
    start = pl.multiple_of(jnp.where(lax.axis_index("row") % 2 == 1, depth, 0), depth)
    copies = [
        pltpu.make_async_copy(source, target, sems.at[i])
        for i, (source, target) in enumerate((
            (p_pattern_hbm, p_pattern),
            (p_hbm, p_ref),
            (ap_pattern_hbm, ap_pattern),
            (ap_hbm.at[pl.ds(start, depth), :], first_ref.at[pl.ds(0, depth), :]),
            (ap_hbm.at[pl.ds(depth - start, depth), :], second_ref.at[pl.ds(0, depth), :]),
        ))
    ]
    for copy in copies:
        copy.start()
    r, c = lax.axis_index("row"), lax.axis_index("col")
    tiles = p_ref.shape[0] // TILE // 2
    half = tiles * TILE
    width = p_ref.shape[1] // TILE
    sources = class_sources(r, cols)
    zeros = jnp.zeros((TILE, TILE), p_ref.dtype)
    line = lax.broadcasted_iota(jnp.int32, (META, TILE), 0)

    def pack(name, odd):
        for out_ref, m in ((keep_ref, int(odd)), (send_ref, 1 - int(odd))):
            for s in range(SLOTS):
                found = [i for mm, i in UNITS[name] if mm == m and slot_of(name, i, odd, width) == s]
                for a in range(tiles):
                    value, row = zeros, m * tiles + a
                    for i in found:
                        tile = p_ref[pl.ds(row * TILE, TILE), pl.ds(i * TILE, TILE)]
                        value = jnp.where(p_pattern[i, row] > 0, tile, value)
                    out_ref[pl.ds(s * half + a * TILE, TILE), :] = value

    def note(odd):
        for out_ref, m in ((keep_ref, int(odd)), (send_ref, 1 - int(odd))):
            value = jnp.zeros((META, TILE), jnp.float32)
            for a in range(tiles):
                for i in range(width):
                    value = jnp.where(line == a * width + i, p_pattern[i, m * tiles + a].astype(jnp.float32), value)
            out_ref[pl.ds(SLOTS * half, META), :] = value.astype(out_ref.dtype)

    copies[0].wait()
    copies[1].wait()
    for odd in (False, True):
        parity = (r % 2 == 1) == odd

        @pl.when(parity)
        def _(odd=odd):
            note(odd)

        for name in range(len(UNITS)):
            @pl.when(parity & (c == sources[name]))
            def _(name=name, odd=odd):
                pack(name, odd)

    @pl.when(functools.reduce(jnp.logical_and, [c != s for s in sources]))
    def _():
        for out in (keep_ref, send_ref):
            out[pl.ds(0, SLOTS * half), :] = jnp.zeros((SLOTS * half, TILE), p_ref.dtype)

    copies[2].wait()
    rows, columns = depth // TILE, first_ref.shape[1] // TILE
    shift = jnp.where(r % 2 == 1, rows, 0)
    for out_ref, low in ((first_ref, shift), (second_ref, rows - shift)):
        for b in range(columns):
            value = jnp.zeros((META, TILE), jnp.float32)
            for a in range(rows):
                value = jnp.where(line == a, ap_pattern[b, low + a].astype(jnp.float32), value)
            out_ref[pl.ds(depth, META), pl.ds(b * TILE, TILE)] = value.astype(out_ref.dtype)
    copies[3].wait()
    copies[4].wait()


def mask_applied(ref, out_ref):
    depth = out_ref.shape[0]
    pattern = ref[pl.ds(depth, META), :].astype(jnp.float32)
    for a in range(depth // TILE):
        weight = jnp.broadcast_to(pattern[a : a + 1, :], (META, out_ref.shape[1])).astype(ref.dtype)
        rows = pl.ds(a * TILE, TILE)
        out_ref[rows, :] = (ref[rows, :].reshape(TILE // META, META, -1) * weight[None]).reshape(TILE, -1)


def mask_kernel(ref, ordered_after, out_ref):
    mask_applied(ref, out_ref)


def mask_own_kernel(first_ref, second_ref, first_out, second_out):
    mask_applied(first_ref, first_out)
    mask_applied(second_ref, second_out)


def merge_kernel(keep_ref, got_ref, half_ref):
    odd = lax.axis_index("row") % 2 == 1
    size = keep_ref.shape[0] - META
    half_ref[pl.ds(0, size), :] = keep_ref[pl.ds(0, size), :] + got_ref[pl.ds(0, size), :]
    mine, theirs = keep_ref[pl.ds(size, META), :], got_ref[pl.ds(size, META), :]
    half_ref[pl.ds(size, META), :] = jnp.where(odd, theirs, mine)
    half_ref[pl.ds(size + META, META), :] = jnp.where(odd, mine, theirs)


def far_forward_kernel(cols, own, cross, ordered_after, out_ref):
    c = lax.axis_index("col")
    inner = (cols == 8) & (c >= 2) & (c < 6)

    @pl.when(inner)
    def _():
        out_ref[...] = cross[...]

    @pl.when(jnp.logical_not(inner))
    def _():
        out_ref[...] = own[...]


def diagonal_forward_kernel(pair, cross, ordered_after, out_ref):
    c = lax.axis_index("col")
    by_pair = (c % 2 == 0) == ((c // 2) % 2 == 0)

    @pl.when(by_pair)
    def _():
        out_ref[...] = pair[...]

    @pl.when(jnp.logical_not(by_pair))
    def _():
        out_ref[...] = cross[...]


def swap_kernel(own, side, pair, cross, own_second, far_first, out_ref):
    size = side.shape[0]
    for j, buffer in enumerate((own, side, pair, cross)):
        for a in range(0, size - 2 * META, TILE):
            out_ref[pl.ds(j * size + a, TILE), :] = buffer[pl.ds(a, TILE), :].T
        out_ref[pl.ds((j + 1) * size - 2 * META, 2 * META), :] = buffer[pl.ds(size - 2 * META, 2 * META), :]
    start = len(FIRST) * size
    for ap in (own_second, far_first):
        for b in range(ap.shape[1] // TILE):
            out_ref[pl.ds(start, ap.shape[0]), :] = ap[:, b * TILE : (b + 1) * TILE]
            start += ap.shape[0]


def pass_kernel(ref, ordered_after, out_ref):
    out_ref[...] = ref[...]


def masked_units(ref, base, flag, odd, slots, half, width, transposed):
    note = base + SLOTS * half + (META if odd else 0)
    pattern = ref[pl.ds(pl.multiple_of(note, META), META), :].astype(jnp.float32)
    pattern = pattern * jnp.where(flag, 1.0, 0.0)
    columns = []
    for i, slot in slots.items():
        tiles = []
        for a in range(half // TILE):
            k = a * width + i
            weight = jnp.broadcast_to(pattern[k : k + 1, :], (META, TILE)).astype(ref.dtype)
            tile = ref[pl.ds(pl.multiple_of(base + slot + a * TILE, META), TILE), :]
            tiles.append((tile.reshape(TILE // META, META, TILE) * weight[None]).reshape(TILE, TILE))
        columns.append(jnp.concatenate(tiles, axis=int(transposed)))
    return jnp.concatenate(columns, axis=1 - int(transposed))


def product(units, ap, transposed):
    contract = (((int(transposed),), (0,)), ((), ()))
    return lax.dot_general(units, ap, contract, preferred_element_type=jnp.float32)


def present(cols, name, kind, valid=True):
    r, c = lax.axis_index("row"), lax.axis_index("col")
    source = class_sources(r, cols)[name]
    return valid & (source >= 0) & (source < cols) & (kind_sources(c, cols)[kind] == source)


def read_applied(name, m, odd, half, size, own, far, swapped, cross_ap):
    depth, rows = 2 * half, pl.ds(m * half, half)
    if name in MAINS:
        return own[int(odd == (name == 0))][rows, :]
    if name in FARS:
        return far[int(odd == (name == 4))][rows, :]
    if odd == (name == 2):
        ref, start = swapped, len(FIRST) * size
    else:
        ref, start = cross_ap, cross_ap.shape[0] - 2 * depth
    return jnp.concatenate([ref[pl.ds(start + b * depth + m * half, half), :] for b in range(2)], axis=1)


def class_units(cols, half, width, odd, name, m, found, kinds, size, mine, theirs):
    here = [present(cols, name, kind) for kind in kinds]
    base = sum(jnp.where(flag, j * size, 0) for j, flag in enumerate(here))
    there = functools.reduce(jnp.logical_or, here)
    slots = {i: slot_of(name, i, odd, width) * half for i in found}
    ref = mine if odd == (m == 1) else theirs
    return masked_units(ref, base, there, odd, slots, half, width, True)


def kind_units(cols, half, width, odd, read, kind, ref, m):
    here = [present(cols, name, kind) for name in range(len(UNITS))]
    there = functools.reduce(jnp.logical_or, here)
    is_far = functools.reduce(jnp.logical_or, [here[name] for name in FARS])
    ap = read(0, m, odd)
    for name in range(1, len(UNITS)):
        ap = jnp.where(here[name], read(name, m, odd), ap)
    slots = {
        i: jnp.where(is_far, slot_of(FARS[0], i, odd, width), slot_of(MAINS[0], i, odd, width)) * half for i in range(width)
    }
    return masked_units(ref, 0, there, odd, slots, half, width, False), ap


def by_parity(body):
    row_odd = lax.axis_index("row") % 2 == 1
    for odd in (False, True):
        @pl.when(row_odd == odd)
        def _(odd=odd):
            body(odd)


def own_kernel(cols, half, width, own_first, own_second, swap, side, c_ref):
    size = side.shape[0]

    def body(odd):
        m = int(odd)
        units = [class_units(cols, half, width, odd, name, m, range(width), FIRST, size, swap, None) for name in MAINS]
        ap = [read_applied(name, m, odd, half, size, (own_first, own_second), None, None, None) for name in MAINS]
        c_ref[...] = product(jnp.concatenate(units, axis=1), jnp.concatenate(ap, axis=0), True)

    by_parity(body)


def near_kernel(cols, half, width, own_first, own_second, far_first, far_second, swapped, cross_ap, swap, diag, far, partial, c_ref):
    size = far.shape[0]
    read = lambda name, m, odd: read_applied(
        name, m, odd, half, size, (own_first, own_second), (far_first, far_second), swapped, cross_ap
    )

    def body(odd):
        mine, theirs = int(odd), 1 - int(odd)
        units = lambda name, m, found: class_units(cols, half, width, odd, name, m, found, FIRST, size, swap, swapped)
        lhs = jnp.concatenate([units(name, theirs, range(width)) for name in MAINS], axis=1)
        rhs = jnp.concatenate([read(name, theirs, odd) for name in MAINS], axis=0)
        c_ref[...] = partial[...] + product(lhs, rhs, True)
        late = [kind_units(cols, half, width, odd, read, kind, ref, mine) for kind, ref in ((DIAG, diag), (FAR, far))]
        lhs, rhs = (jnp.concatenate(x, axis=0) for x in zip(*late))
        c_ref[...] += product(lhs, rhs, False)
        for name in NEARS:
            found = sorted({i for _, i in UNITS[name]})
            lhs = jnp.concatenate([units(name, m, found) for m in range(2)], axis=1)
            rhs = jnp.concatenate([read(name, m, odd) for m in range(2)], axis=0)
            c_ref[pl.ds(found[0] * TILE, len(found) * TILE), :] += product(lhs, rhs, True)
        for name in FARS:
            for m, i in UNITS[name]:
                c_ref[pl.ds(i * TILE, TILE), :] += product(units(name, m, [i]), read(name, m, odd), True)

    by_parity(body)


def diagonal_kernel(cols, half, width, own_first, own_second, far_first, far_second, swapped, cross_ap, diag_last, partial, c_ref):
    size = diag_last.shape[0]
    read = lambda name, m, odd: read_applied(
        name, m, odd, half, size, (own_first, own_second), (far_first, far_second), swapped, cross_ap
    )

    def body(odd):
        c_ref[...] = partial[...] + product(*kind_units(cols, half, width, odd, read, DIAG, diag_last, 1 - int(odd)), False)

    by_parity(body)


def last_kernel(cols, half, width, own_first, own_second, far_first, far_second, swapped, cross_ap, far_last, partial, out_hbm, c_ref, sems):
    size = far_last.shape[0]
    read = lambda name, m, odd: read_applied(
        name, m, odd, half, size, (own_first, own_second), (far_first, far_second), swapped, cross_ap
    )

    def body(odd):
        units, ap = kind_units(cols, half, width, odd, read, FAR, far_last, 1 - int(odd))
        copies = []
        for i in range(width):
            rows = pl.ds(i * TILE, TILE)
            c_ref[rows, :] = partial[rows, :] + product(units[:, i * TILE : (i + 1) * TILE], ap, False)
            copies.append(pltpu.make_async_copy(c_ref.at[rows, :], out_hbm.at[rows, :], sems.at[i]))
            copies[-1].start()
        for copy in copies:
            copy.wait()

    by_parity(body)


def on_device(rows, cols, prolong, applied, prolong_pattern, applied_pattern):
    depth, width = prolong.shape[0], prolong.shape[1] // TILE
    half = depth // 2
    data = SLOTS * half
    size = data + 2 * META
    vmem = pl.BlockSpec(memory_space=pltpu.VMEM)
    smem = pl.BlockSpec(memory_space=pltpu.SMEM)
    params = pltpu.CompilerParams(vmem_limit_bytes=24 << 20)
    shape = lambda *s: jax.ShapeDtypeStruct(s, prolong.dtype)

    def call(kernel, name, out_shape, *operands, specs=None, weight=0, **more):
        if weight:
            more["cost_estimate"] = pl.CostEstimate(flops=weight * 1_000_000_000, bytes_accessed=weight * 3_000_000, transcendentals=0)
        out_specs = (vmem,) * len(out_shape) if isinstance(out_shape, tuple) else vmem
        return pl.pallas_call(
            kernel, out_shape=out_shape, in_specs=specs or [vmem] * len(operands), out_specs=out_specs,
            compiler_params=params, name=name, **more,
        )(*operands)

    def move(x, pairs):
        return lax.ppermute(x, AXES, pairs)

    def row_pairs(pairs):
        return [(a * cols + c, b * cols + c) for a, b in pairs for c in range(cols)]

    def col_pairs(pairs):
        return [(r * cols + a, r * cols + b) for r in range(rows) for a, b in pairs if 0 <= b < cols]

    partner = row_pairs([(r, r ^ 1) for r in range(rows)])
    opposite = [(r, (r + rows // 2) % rows) for r in range(rows)]

    hbm = pl.BlockSpec(memory_space=pltpu.HBM)
    half_ap = shape(depth, applied.shape[1])
    keep, send, raw_first, raw_second = call(
        functools.partial(prepare_kernel, cols), "prepare",
        (shape(data + META, TILE),) * 2 + (shape(depth + META, applied.shape[1]),) * 2,
        *[pltpu.with_memory_space_constraint(x, pltpu.HBM) for x in (prolong, applied, prolong_pattern.T, applied_pattern.T)],
        specs=[hbm] * 4,
        scratch_shapes=[
            pltpu.VMEM(prolong.shape, prolong.dtype),
            pltpu.SMEM(prolong_pattern.shape[::-1], jnp.int32),
            pltpu.SMEM(applied_pattern.shape[::-1], jnp.int32),
            pltpu.SemaphoreType.DMA((5,)),
        ],
    )
    got = move(send, partner)
    far_first, far_second = move(raw_first, row_pairs(opposite)), move(raw_second, row_pairs(opposite))
    mine = call(merge_kernel, "merge", shape(size, TILE), keep, got)
    middle = lambda c: 2 <= c < cols - 2
    step = lambda c: c - 2 if (c // 2) % 2 == 0 else c + 2
    cross = move(mine, [
        (r * cols + c, r * cols + step(c) if middle(c) else (r ^ 1) * cols + c) for r in range(rows) for c in range(cols)
    ])
    pair = move(mine, col_pairs([(c, c ^ 2) for c in range(cols)]))
    side = move(mine, col_pairs([(c, c ^ 1) for c in range(cols)]))

    if cols == 8:
        far_pairs = [(0, 4), (1, 5), (2, 0), (3, 1), (4, 6), (5, 7), (6, 2), (7, 3)]
    else:
        far_pairs = [(c, (c + cols // 2) % cols) for c in range(cols)]
    diag_send = call(diagonal_forward_kernel, "diagonal_forward", shape(size, TILE), pair, cross, pair)
    diag = move(diag_send, col_pairs([(c, c ^ 1) for c in range(cols)]))
    far_send = call(
        functools.partial(far_forward_kernel, cols), "far_forward", shape(size, TILE), mine, cross, cross
    )
    far = move(far_send, col_pairs(far_pairs))
    own_first, own_second = call(mask_own_kernel, "mask_own", (half_ap,) * 2, raw_first, raw_second)
    far_first = call(mask_kernel, "settle_first", half_ap, far_first, mine, weight=FIRST_WEIGHT)
    swap = call(
        swap_kernel, "swap", shape(len(FIRST) * size + 4 * depth, TILE), mine, side, pair, cross, own_second, far_first
    )
    swapped = move(swap, partner)
    result = jax.ShapeDtypeStruct((prolong.shape[1], applied.shape[1]), jnp.float32)
    sizes = (cols, half, width)
    partial = call(functools.partial(own_kernel, *sizes), "own", result, own_first, own_second, swap, side)
    far_second = call(mask_kernel, "settle", half_ap, far_second, partial)
    diag_last = move(call(pass_kernel, "pass_diagonal", shape(size, TILE), diag, diag_send), partner)
    far_last = move(call(pass_kernel, "pass_far", shape(size, TILE), far, far_second, weight=LAST_WEIGHT), partner)
    beyond = [(r, r + 1 if r % 2 == 1 else r - 1) for r in range(rows)]
    relay = [((r + rows // 2) % rows, t) for r, t in beyond if 0 <= t < rows]
    if all(h ^ 1 == t for h, t in relay):
        cross_ap = swapped
    else:
        first = own_first.reshape(depth, 2, TILE).transpose(1, 0, 2).reshape(2 * depth, TILE)
        cross_ap = move(first, row_pairs([(r, t) for r, t in beyond if 0 <= t < rows]))

    aps = (own_first, own_second, far_first, far_second, swapped, cross_ap)
    partial = call(functools.partial(near_kernel, *sizes), "near", result, *aps, swap, diag, far, partial)
    partial = call(functools.partial(diagonal_kernel, *sizes), "diagonal", result, *aps, diag_last, partial)
    operands = (*aps, far_last, partial)
    return pl.pallas_call(
        functools.partial(last_kernel, *sizes), out_shape=result, in_specs=[vmem] * len(operands), out_specs=hbm,
        compiler_params=params, name="last",
        scratch_shapes=[pltpu.VMEM(result.shape, jnp.float32), pltpu.SemaphoreType.DMA((width,))],
    )(*operands)


def solution(mesh):
    in_specs = (P("col", "row"), P("row", "col"), P("col", "row"), P("row", "col"))
    return jax.shard_map(
        functools.partial(on_device, mesh.shape["row"], mesh.shape["col"]),
        mesh=mesh, in_specs=in_specs, out_specs=P("row", "col"), check_vma=False,
    )
```

```python
import functools

import jax
import jax.numpy as jnp
from jax import lax
from jax.experimental import pallas as pl
from jax.experimental.pallas import tpu as pltpu
from jax.sharding import PartitionSpec as P

TILE = 128
AXES = ("row", "col")
LAST_WEIGHT, FIRST_WEIGHT = 20, 5
DIAGONAL_FIRST = 0
SLOTS = 3
META = 16
MAINS, NEARS, FARS = (0, 1), (2, 3), (4, 5)
UNITS = (
    ((0, 0), (0, 1), (0, 2), (1, 0), (1, 1), (1, 2), (1, 3)),
    ((0, 0), (0, 1), (0, 2), (0, 3), (1, 1), (1, 2), (1, 3)),
    ((0, 0), (1, 0), (1, 1)),
    ((0, 2), (0, 3), (1, 3)),
    ((0, 0), (1, 1)),
    ((0, 2), (1, 3)),
)
OWN, SIDE, PAIR, CROSS, FAR, DIAG = range(6)
FIRST, SECOND = (OWN, SIDE, PAIR, CROSS), (FAR, DIAG)


def class_sources(r, cols):
    rem = lambda x: lax.rem(x, cols)
    return (2 * r, 2 * r + 1, 2 * r - 1, 2 * r + 2, rem(2 * r + cols // 2), rem(2 * r + 1 + cols // 2))


def kind_sources(c, cols):
    even, low = c % 2 == 0, (c // 2) % 2 == 0
    near, past = jnp.where(even, c + 1, c - 1), jnp.where(even, c - 1, c + 1)
    pair, across = jnp.where(low, c + 2, c - 2), jnp.where(low, c - 2, c + 2)
    return {OWN: c, SIDE: near, PAIR: pair, CROSS: across, FAR: lax.rem(c + cols // 2, cols), DIAG: past}


def slot_of(name, i, odd, width):
    return 2 if name in FARS else (i + (width if odd else 0)) % SLOTS


def prepare_kernel(cols, p_hbm, ap_hbm, p_pattern_hbm, ap_pattern_hbm, keep_ref, send_ref, first_ref, second_ref, p_ref, p_pattern, ap_pattern, sems):
    depth = p_ref.shape[0]
    start = pl.multiple_of(jnp.where(lax.axis_index("row") % 2 == 1, depth, 0), depth)
    copies = [
        pltpu.make_async_copy(source, target, sems.at[i])
        for i, (source, target) in enumerate((
            (p_pattern_hbm, p_pattern),
            (p_hbm, p_ref),
            (ap_pattern_hbm, ap_pattern),
            (ap_hbm.at[pl.ds(start, depth), :], first_ref.at[pl.ds(0, depth), :]),
            (ap_hbm.at[pl.ds(depth - start, depth), :], second_ref.at[pl.ds(0, depth), :]),
        ))
    ]
    for copy in copies:
        copy.start()
    r, c = lax.axis_index("row"), lax.axis_index("col")
    tiles = p_ref.shape[0] // TILE // 2
    half = tiles * TILE
    width = p_ref.shape[1] // TILE
    sources = class_sources(r, cols)
    zeros = jnp.zeros((TILE, TILE), p_ref.dtype)
    line = lax.broadcasted_iota(jnp.int32, (META, TILE), 0)

    def pack(name, odd):
        for out_ref, m in ((keep_ref, int(odd)), (send_ref, 1 - int(odd))):
            for s in range(SLOTS):
                found = [i for mm, i in UNITS[name] if mm == m and slot_of(name, i, odd, width) == s]
                for a in range(tiles):
                    value, row = zeros, m * tiles + a
                    for i in found:
                        tile = p_ref[pl.ds(row * TILE, TILE), pl.ds(i * TILE, TILE)]
                        value = jnp.where(p_pattern[i, row] > 0, tile, value)
                    out_ref[pl.ds(s * half + a * TILE, TILE), :] = value

    def note(odd):
        for out_ref, m in ((keep_ref, int(odd)), (send_ref, 1 - int(odd))):
            value = jnp.zeros((META, TILE), jnp.float32)
            for a in range(tiles):
                for i in range(width):
                    value = jnp.where(line == a * width + i, p_pattern[i, m * tiles + a].astype(jnp.float32), value)
            out_ref[pl.ds(SLOTS * half, META), :] = value.astype(out_ref.dtype)

    copies[0].wait()
    copies[1].wait()
    for odd in (False, True):
        parity = (r % 2 == 1) == odd

        @pl.when(parity)
        def _(odd=odd):
            note(odd)

        for name in range(len(UNITS)):
            @pl.when(parity & (c == sources[name]))
            def _(name=name, odd=odd):
                pack(name, odd)

    @pl.when(functools.reduce(jnp.logical_and, [c != s for s in sources]))
    def _():
        for out in (keep_ref, send_ref):
            out[pl.ds(0, SLOTS * half), :] = jnp.zeros((SLOTS * half, TILE), p_ref.dtype)

    copies[2].wait()
    rows, columns = depth // TILE, first_ref.shape[1] // TILE
    shift = jnp.where(r % 2 == 1, rows, 0)
    for out_ref, low in ((first_ref, shift), (second_ref, rows - shift)):
        for b in range(columns):
            value = jnp.zeros((META, TILE), jnp.float32)
            for a in range(rows):
                value = jnp.where(line == a, ap_pattern[b, low + a].astype(jnp.float32), value)
            out_ref[pl.ds(depth, META), pl.ds(b * TILE, TILE)] = value.astype(out_ref.dtype)
    copies[3].wait()
    copies[4].wait()


def mask_applied(ref, out_ref):
    depth = out_ref.shape[0]
    pattern = ref[pl.ds(depth, META), :].astype(jnp.float32)
    for a in range(depth // TILE):
        weight = jnp.broadcast_to(pattern[a : a + 1, :], (META, out_ref.shape[1])).astype(ref.dtype)
        rows = pl.ds(a * TILE, TILE)
        out_ref[rows, :] = (ref[rows, :].reshape(TILE // META, META, -1) * weight[None]).reshape(TILE, -1)


def mask_kernel(ref, ordered_after, out_ref):
    mask_applied(ref, out_ref)


def mask_own_kernel(first_ref, second_ref, first_out, second_out):
    mask_applied(first_ref, first_out)
    mask_applied(second_ref, second_out)


def merge_kernel(keep_ref, got_ref, half_ref):
    odd = lax.axis_index("row") % 2 == 1
    size = keep_ref.shape[0] - META
    half_ref[pl.ds(0, size), :] = keep_ref[pl.ds(0, size), :] + got_ref[pl.ds(0, size), :]
    mine, theirs = keep_ref[pl.ds(size, META), :], got_ref[pl.ds(size, META), :]
    half_ref[pl.ds(size, META), :] = jnp.where(odd, theirs, mine)
    half_ref[pl.ds(size + META, META), :] = jnp.where(odd, mine, theirs)


def late_kind(step, odd):
    return DIAG if odd == (DIAGONAL_FIRST != step) else FAR


def forward_kernel(cols, step, own, pair, cross, ordered_after, out_ref):
    row_odd, c = lax.axis_index("row") % 2 == 1, lax.axis_index("col")
    diagonal = row_odd == (late_kind(step, True) == DIAG)
    by_pair = (c % 2 == 0) == ((c // 2) % 2 == 0)
    inner = (cols == 8) & (c >= 2) & (c < 6)
    from_pair = diagonal & by_pair
    from_own = jnp.logical_not(diagonal | inner)

    @pl.when(from_pair)
    def _():
        out_ref[...] = pair[...]

    @pl.when(from_own)
    def _():
        out_ref[...] = own[...]

    @pl.when(jnp.logical_not(from_pair | from_own))
    def _():
        out_ref[...] = cross[...]


def swap_kernel(own, side, pair, cross, own_second, far_first, out_ref):
    size = side.shape[0]
    for j, buffer in enumerate((own, side, pair, cross)):
        for a in range(0, size - 2 * META, TILE):
            out_ref[pl.ds(j * size + a, TILE), :] = buffer[pl.ds(a, TILE), :].T
        out_ref[pl.ds((j + 1) * size - 2 * META, 2 * META), :] = buffer[pl.ds(size - 2 * META, 2 * META), :]
    start = len(FIRST) * size
    for ap in (own_second, far_first):
        for b in range(ap.shape[1] // TILE):
            out_ref[pl.ds(start, ap.shape[0]), :] = ap[:, b * TILE : (b + 1) * TILE]
            start += ap.shape[0]


def pass_kernel(ref, ordered_after, out_ref):
    out_ref[...] = ref[...]


def masked_units(ref, base, flag, odd, slots, half, width, transposed):
    note = base + SLOTS * half + (META if odd else 0)
    pattern = ref[pl.ds(pl.multiple_of(note, META), META), :].astype(jnp.float32)
    pattern = pattern * jnp.where(flag, 1.0, 0.0)
    columns = []
    for i, slot in slots.items():
        tiles = []
        for a in range(half // TILE):
            k = a * width + i
            weight = jnp.broadcast_to(pattern[k : k + 1, :], (META, TILE)).astype(ref.dtype)
            tile = ref[pl.ds(pl.multiple_of(base + slot + a * TILE, META), TILE), :]
            tiles.append((tile.reshape(TILE // META, META, TILE) * weight[None]).reshape(TILE, TILE))
        columns.append(jnp.concatenate(tiles, axis=int(transposed)))
    return jnp.concatenate(columns, axis=1 - int(transposed))


def product(units, ap, transposed):
    contract = (((int(transposed),), (0,)), ((), ()))
    return lax.dot_general(units, ap, contract, preferred_element_type=jnp.float32)


def present(cols, name, kind, valid=True):
    r, c = lax.axis_index("row"), lax.axis_index("col")
    source = class_sources(r, cols)[name]
    return valid & (source >= 0) & (source < cols) & (kind_sources(c, cols)[kind] == source)


def read_applied(name, m, odd, half, size, own, far, swapped, cross_ap):
    depth, rows = 2 * half, pl.ds(m * half, half)
    if name in MAINS:
        return own[int(odd == (name == 0))][rows, :]
    if name in FARS:
        return far[int(odd == (name == 4))][rows, :]
    if odd == (name == 2):
        ref, start = swapped, len(FIRST) * size
    else:
        ref, start = cross_ap, cross_ap.shape[0] - 2 * depth
    return jnp.concatenate([ref[pl.ds(start + b * depth + m * half, half), :] for b in range(2)], axis=1)


def class_units(cols, half, width, odd, name, m, found, kinds, size, mine, theirs):
    here = [present(cols, name, kind) for kind in kinds]
    base = sum(jnp.where(flag, j * size, 0) for j, flag in enumerate(here))
    there = functools.reduce(jnp.logical_or, here)
    slots = {i: slot_of(name, i, odd, width) * half for i in found}
    ref = mine if odd == (m == 1) else theirs
    return masked_units(ref, base, there, odd, slots, half, width, True)


def kind_units(cols, half, width, odd, read, kind, ref, m):
    here = [present(cols, name, kind) for name in range(len(UNITS))]
    there = functools.reduce(jnp.logical_or, here)
    is_far = functools.reduce(jnp.logical_or, [here[name] for name in FARS])
    ap = read(0, m, odd)
    for name in range(1, len(UNITS)):
        ap = jnp.where(here[name], read(name, m, odd), ap)
    slots = {
        i: jnp.where(is_far, slot_of(FARS[0], i, odd, width), slot_of(MAINS[0], i, odd, width)) * half for i in range(width)
    }
    return masked_units(ref, 0, there, odd, slots, half, width, False), ap


def by_parity(body):
    row_odd = lax.axis_index("row") % 2 == 1
    for odd in (False, True):
        @pl.when(row_odd == odd)
        def _(odd=odd):
            body(odd)


def own_kernel(cols, half, width, own_first, own_second, swap, side, c_ref):
    size = side.shape[0]

    def body(odd):
        m = int(odd)
        units = [class_units(cols, half, width, odd, name, m, range(width), FIRST, size, swap, None) for name in MAINS]
        ap = [read_applied(name, m, odd, half, size, (own_first, own_second), None, None, None) for name in MAINS]
        c_ref[...] = product(jnp.concatenate(units, axis=1), jnp.concatenate(ap, axis=0), True)

    by_parity(body)


def near_kernel(cols, half, width, own_first, own_second, far_first, far_second, swapped, cross_ap, swap, late_first, late_second, partial, c_ref):
    size = late_first.shape[0]
    read = lambda name, m, odd: read_applied(
        name, m, odd, half, size, (own_first, own_second), (far_first, far_second), swapped, cross_ap
    )

    def body(odd):
        mine, theirs = int(odd), 1 - int(odd)
        units = lambda name, m, found: class_units(cols, half, width, odd, name, m, found, FIRST, size, swap, swapped)
        lhs = jnp.concatenate([units(name, theirs, range(width)) for name in MAINS], axis=1)
        rhs = jnp.concatenate([read(name, theirs, odd) for name in MAINS], axis=0)
        c_ref[...] = partial[...] + product(lhs, rhs, True)
        late = [
            kind_units(cols, half, width, odd, read, late_kind(step, odd), ref, mine)
            for step, ref in enumerate((late_first, late_second))
        ]
        lhs, rhs = (jnp.concatenate(x, axis=0) for x in zip(*late))
        c_ref[...] += product(lhs, rhs, False)
        for name in NEARS:
            found = sorted({i for _, i in UNITS[name]})
            lhs = jnp.concatenate([units(name, m, found) for m in range(2)], axis=1)
            rhs = jnp.concatenate([read(name, m, odd) for m in range(2)], axis=0)
            c_ref[pl.ds(found[0] * TILE, len(found) * TILE), :] += product(lhs, rhs, True)
        for name in FARS:
            for m, i in UNITS[name]:
                c_ref[pl.ds(i * TILE, TILE), :] += product(units(name, m, [i]), read(name, m, odd), True)

    by_parity(body)


def late_kernel(cols, half, width, own_first, own_second, far_first, far_second, swapped, cross_ap, late_first, partial, c_ref):
    size = late_first.shape[0]
    read = lambda name, m, odd: read_applied(
        name, m, odd, half, size, (own_first, own_second), (far_first, far_second), swapped, cross_ap
    )

    def body(odd):
        c_ref[...] = partial[...] + product(*kind_units(cols, half, width, odd, read, late_kind(0, not odd), late_first, 1 - int(odd)), False)

    by_parity(body)


def last_kernel(cols, half, width, own_first, own_second, far_first, far_second, swapped, cross_ap, late_second, partial, out_hbm, c_ref, sems):
    size = late_second.shape[0]
    read = lambda name, m, odd: read_applied(
        name, m, odd, half, size, (own_first, own_second), (far_first, far_second), swapped, cross_ap
    )

    def body(odd):
        units, ap = kind_units(cols, half, width, odd, read, late_kind(1, not odd), late_second, 1 - int(odd))
        copies = []
        for i in range(width):
            rows = pl.ds(i * TILE, TILE)
            c_ref[rows, :] = partial[rows, :] + product(units[:, i * TILE : (i + 1) * TILE], ap, False)
            copies.append(pltpu.make_async_copy(c_ref.at[rows, :], out_hbm.at[rows, :], sems.at[i]))
            copies[-1].start()
        for copy in copies:
            copy.wait()

    by_parity(body)


def on_device(rows, cols, prolong, applied, prolong_pattern, applied_pattern):
    depth, width = prolong.shape[0], prolong.shape[1] // TILE
    half = depth // 2
    data = SLOTS * half
    size = data + 2 * META
    vmem = pl.BlockSpec(memory_space=pltpu.VMEM)
    smem = pl.BlockSpec(memory_space=pltpu.SMEM)
    params = pltpu.CompilerParams(vmem_limit_bytes=24 << 20)
    shape = lambda *s: jax.ShapeDtypeStruct(s, prolong.dtype)

    def call(kernel, name, out_shape, *operands, specs=None, weight=0, **more):
        if weight:
            more["cost_estimate"] = pl.CostEstimate(flops=weight * 1_000_000_000, bytes_accessed=weight * 3_000_000, transcendentals=0)
        out_specs = (vmem,) * len(out_shape) if isinstance(out_shape, tuple) else vmem
        return pl.pallas_call(
            kernel, out_shape=out_shape, in_specs=specs or [vmem] * len(operands), out_specs=out_specs,
            compiler_params=params, name=name, **more,
        )(*operands)

    def move(x, pairs):
        return lax.ppermute(x, AXES, pairs)

    def row_pairs(pairs):
        return [(a * cols + c, b * cols + c) for a, b in pairs for c in range(cols)]

    def col_pairs(pairs):
        return [(r * cols + a, r * cols + b) for r in range(rows) for a, b in pairs if 0 <= b < cols]

    partner = row_pairs([(r, r ^ 1) for r in range(rows)])
    opposite = [(r, (r + rows // 2) % rows) for r in range(rows)]

    hbm = pl.BlockSpec(memory_space=pltpu.HBM)
    half_ap = shape(depth, applied.shape[1])
    keep, send, raw_first, raw_second = call(
        functools.partial(prepare_kernel, cols), "prepare",
        (shape(data + META, TILE),) * 2 + (shape(depth + META, applied.shape[1]),) * 2,
        *[pltpu.with_memory_space_constraint(x, pltpu.HBM) for x in (prolong, applied, prolong_pattern.T, applied_pattern.T)],
        specs=[hbm] * 4,
        scratch_shapes=[
            pltpu.VMEM(prolong.shape, prolong.dtype),
            pltpu.SMEM(prolong_pattern.shape[::-1], jnp.int32),
            pltpu.SMEM(applied_pattern.shape[::-1], jnp.int32),
            pltpu.SemaphoreType.DMA((5,)),
        ],
    )
    got = move(send, partner)
    far_first, far_second = move(raw_first, row_pairs(opposite)), move(raw_second, row_pairs(opposite))
    mine = call(merge_kernel, "merge", shape(size, TILE), keep, got)
    middle = lambda c: 2 <= c < cols - 2
    step = lambda c: c - 2 if (c // 2) % 2 == 0 else c + 2
    cross = move(mine, [
        (r * cols + c, r * cols + step(c) if middle(c) else (r ^ 1) * cols + c) for r in range(rows) for c in range(cols)
    ])
    pair = move(mine, col_pairs([(c, c ^ 2) for c in range(cols)]))
    side = move(mine, col_pairs([(c, c ^ 1) for c in range(cols)]))

    if cols == 8:
        far_pairs = [(0, 4), (1, 5), (2, 0), (3, 1), (4, 6), (5, 7), (6, 2), (7, 3)]
    else:
        far_pairs = [(c, (c + cols // 2) % cols) for c in range(cols)]
    def relay_pairs(step):
        pairs = {DIAG: [(c, c ^ 1) for c in range(cols)], FAR: far_pairs}
        return [(r * cols + a, r * cols + b) for r in range(rows) for a, b in pairs[late_kind(step, r % 2 == 1)]]

    late, after = [], cross
    for step in range(2):
        send_on = call(
            functools.partial(forward_kernel, cols, step), "forward", shape(size, TILE), mine, pair, cross, after
        )
        late.append(move(send_on, relay_pairs(step)))
        after = send_on
    own_first, own_second = call(mask_own_kernel, "mask_own", (half_ap,) * 2, raw_first, raw_second)
    far_first = call(mask_kernel, "settle_first", half_ap, far_first, mine, weight=FIRST_WEIGHT)
    swap = call(
        swap_kernel, "swap", shape(len(FIRST) * size + 4 * depth, TILE), mine, side, pair, cross, own_second, far_first
    )
    swapped = move(swap, partner)
    result = jax.ShapeDtypeStruct((prolong.shape[1], applied.shape[1]), jnp.float32)
    sizes = (cols, half, width)
    partial = call(functools.partial(own_kernel, *sizes), "own", result, own_first, own_second, swap, side)
    far_second = call(mask_kernel, "settle", half_ap, far_second, partial)
    late_first = move(call(pass_kernel, "pass_late", shape(size, TILE), late[0], mine), partner)
    late_second = move(call(pass_kernel, "pass_late", shape(size, TILE), late[1], far_second, weight=LAST_WEIGHT), partner)
    beyond = [(r, r + 1 if r % 2 == 1 else r - 1) for r in range(rows)]
    relay = [((r + rows // 2) % rows, t) for r, t in beyond if 0 <= t < rows]
    if all(h ^ 1 == t for h, t in relay):
        cross_ap = swapped
    else:
        first = own_first.reshape(depth, 2, TILE).transpose(1, 0, 2).reshape(2 * depth, TILE)
        cross_ap = move(first, row_pairs([(r, t) for r, t in beyond if 0 <= t < rows]))

    aps = (own_first, own_second, far_first, far_second, swapped, cross_ap)
    partial = call(functools.partial(near_kernel, *sizes), "near", result, *aps, swap, *late, partial)
    partial = call(functools.partial(late_kernel, *sizes), "late", result, *aps, late_first, partial)
    operands = (*aps, late_second, partial)
    return pl.pallas_call(
        functools.partial(last_kernel, *sizes), out_shape=result, in_specs=[vmem] * len(operands), out_specs=hbm,
        compiler_params=params, name="last",
        scratch_shapes=[pltpu.VMEM(result.shape, jnp.float32), pltpu.SemaphoreType.DMA((width,))],
    )(*operands)


def solution(mesh):
    in_specs = (P("col", "row"), P("row", "col"), P("col", "row"), P("row", "col"))
    return jax.shard_map(
        functools.partial(on_device, mesh.shape["row"], mesh.shape["col"]),
        mesh=mesh, in_specs=in_specs, out_specs=P("row", "col"), check_vma=False,
    )
```

```python
import functools

import jax
import jax.numpy as jnp
from jax import lax
from jax.experimental import pallas as pl
from jax.experimental.pallas import tpu as pltpu
from jax.sharding import PartitionSpec as P

TILE = 128
AXES = ("row", "col")
LAST_WEIGHT, FIRST_WEIGHT = 20, 5
DIAGONAL_FIRST = 0
SLOTS = 3
META = 16
MAINS, NEARS, FARS = (0, 1), (2, 3), (4, 5)
UNITS = (
    ((0, 0), (0, 1), (0, 2), (1, 0), (1, 1), (1, 2), (1, 3)),
    ((0, 0), (0, 1), (0, 2), (0, 3), (1, 1), (1, 2), (1, 3)),
    ((0, 0), (1, 0), (1, 1)),
    ((0, 2), (0, 3), (1, 3)),
    ((0, 0), (1, 1)),
    ((0, 2), (1, 3)),
)
OWN, SIDE, PAIR, CROSS, FAR, DIAG = range(6)
FIRST, SECOND = (OWN, SIDE, PAIR, CROSS), (FAR, DIAG)


def class_sources(r, cols):
    rem = lambda x: lax.rem(x, cols)
    return (2 * r, 2 * r + 1, 2 * r - 1, 2 * r + 2, rem(2 * r + cols // 2), rem(2 * r + 1 + cols // 2))


def kind_sources(c, cols):
    even, low = c % 2 == 0, (c // 2) % 2 == 0
    near, past = jnp.where(even, c + 1, c - 1), jnp.where(even, c - 1, c + 1)
    pair, across = jnp.where(low, c + 2, c - 2), jnp.where(low, c - 2, c + 2)
    return {OWN: c, SIDE: near, PAIR: pair, CROSS: across, FAR: lax.rem(c + cols // 2, cols), DIAG: past}


def slot_of(name, i, odd, width):
    return 2 if name in FARS else (i + (width if odd else 0)) % SLOTS


def prepare_kernel(cols, p_hbm, ap_hbm, p_pattern_hbm, ap_pattern_hbm, keep_ref, send_ref, first_ref, second_ref, p_ref, p_pattern, ap_pattern, sems):
    depth = p_ref.shape[0]
    start = pl.multiple_of(jnp.where(lax.axis_index("row") % 2 == 1, depth, 0), depth)
    copies = [
        pltpu.make_async_copy(source, target, sems.at[i])
        for i, (source, target) in enumerate((
            (p_pattern_hbm, p_pattern),
            (p_hbm, p_ref),
            (ap_pattern_hbm, ap_pattern),
            (ap_hbm.at[pl.ds(start, depth), :], first_ref.at[pl.ds(0, depth), :]),
            (ap_hbm.at[pl.ds(depth - start, depth), :], second_ref.at[pl.ds(0, depth), :]),
        ))
    ]
    for copy in copies:
        copy.start()
    r, c = lax.axis_index("row"), lax.axis_index("col")
    tiles = p_ref.shape[0] // TILE // 2
    half = tiles * TILE
    width = p_ref.shape[1] // TILE
    sources = class_sources(r, cols)
    zeros = jnp.zeros((TILE, TILE), p_ref.dtype)
    line = lax.broadcasted_iota(jnp.int32, (META, TILE), 0)

    def pack(name, odd):
        for out_ref, m in ((keep_ref, int(odd)), (send_ref, 1 - int(odd))):
            for s in range(SLOTS):
                found = [i for mm, i in UNITS[name] if mm == m and slot_of(name, i, odd, width) == s]
                for a in range(tiles):
                    value, row = zeros, m * tiles + a
                    for i in found:
                        tile = p_ref[pl.ds(row * TILE, TILE), pl.ds(i * TILE, TILE)]
                        value = jnp.where(p_pattern[i, row] > 0, tile, value)
                    out_ref[pl.ds(s * half + a * TILE, TILE), :] = value

    def note(odd):
        for out_ref, m in ((keep_ref, int(odd)), (send_ref, 1 - int(odd))):
            value = jnp.zeros((META, TILE), jnp.float32)
            for a in range(tiles):
                for i in range(width):
                    value = jnp.where(line == a * width + i, p_pattern[i, m * tiles + a].astype(jnp.float32), value)
            out_ref[pl.ds(SLOTS * half, META), :] = value.astype(out_ref.dtype)

    copies[0].wait()
    copies[1].wait()
    for odd in (False, True):
        parity = (r % 2 == 1) == odd

        @pl.when(parity)
        def _(odd=odd):
            note(odd)

        for name in range(len(UNITS)):
            @pl.when(parity & (c == sources[name]))
            def _(name=name, odd=odd):
                pack(name, odd)

    @pl.when(functools.reduce(jnp.logical_and, [c != s for s in sources]))
    def _():
        for out in (keep_ref, send_ref):
            out[pl.ds(0, SLOTS * half), :] = jnp.zeros((SLOTS * half, TILE), p_ref.dtype)

    copies[2].wait()
    rows, columns = depth // TILE, first_ref.shape[1] // TILE
    shift = jnp.where(r % 2 == 1, rows, 0)
    for out_ref, low in ((first_ref, shift), (second_ref, rows - shift)):
        for b in range(columns):
            value = jnp.zeros((META, TILE), jnp.float32)
            for a in range(rows):
                value = jnp.where(line == a, ap_pattern[b, low + a].astype(jnp.float32), value)
            out_ref[pl.ds(depth, META), pl.ds(b * TILE, TILE)] = value.astype(out_ref.dtype)
    copies[3].wait()
    copies[4].wait()


def mask_applied(ref, out_ref):
    depth = out_ref.shape[0]
    pattern = ref[pl.ds(depth, META), :].astype(jnp.float32)
    for a in range(depth // TILE):
        weight = jnp.broadcast_to(pattern[a : a + 1, :], (META, out_ref.shape[1])).astype(ref.dtype)
        rows = pl.ds(a * TILE, TILE)
        out_ref[rows, :] = (ref[rows, :].reshape(TILE // META, META, -1) * weight[None]).reshape(TILE, -1)


def mask_kernel(ref, ordered_after, out_ref):
    mask_applied(ref, out_ref)


def mask_own_kernel(first_ref, second_ref, first_out, second_out):
    mask_applied(first_ref, first_out)
    mask_applied(second_ref, second_out)


def merge_kernel(keep_ref, got_ref, half_ref):
    odd = lax.axis_index("row") % 2 == 1
    size = keep_ref.shape[0] - META
    half_ref[pl.ds(0, size), :] = keep_ref[pl.ds(0, size), :] + got_ref[pl.ds(0, size), :]
    mine, theirs = keep_ref[pl.ds(size, META), :], got_ref[pl.ds(size, META), :]
    half_ref[pl.ds(size, META), :] = jnp.where(odd, theirs, mine)
    half_ref[pl.ds(size + META, META), :] = jnp.where(odd, mine, theirs)


def late_kind(step, odd):
    return DIAG if odd == (DIAGONAL_FIRST != step) else FAR


def forward_kernel(cols, step, own, pair, cross, ordered_after, out_ref):
    row_odd, c = lax.axis_index("row") % 2 == 1, lax.axis_index("col")
    diagonal = row_odd == (late_kind(step, True) == DIAG)
    by_pair = (c % 2 == 0) == ((c // 2) % 2 == 0)
    inner = (cols == 8) & (c >= 2) & (c < 6)
    from_pair = diagonal & by_pair
    from_own = jnp.logical_not(diagonal | inner)

    @pl.when(from_pair)
    def _():
        out_ref[...] = pair[...]

    @pl.when(from_own)
    def _():
        out_ref[...] = own[...]

    @pl.when(jnp.logical_not(from_pair | from_own))
    def _():
        out_ref[...] = cross[...]


def swap_kernel(own, side, pair, cross, own_second, far_first, out_ref):
    size = side.shape[0]
    for j, buffer in enumerate((own, side, pair, cross)):
        for a in range(0, size - 2 * META, TILE):
            out_ref[pl.ds(j * size + a, TILE), :] = buffer[pl.ds(a, TILE), :].T
        out_ref[pl.ds((j + 1) * size - 2 * META, 2 * META), :] = buffer[pl.ds(size - 2 * META, 2 * META), :]
    start = len(FIRST) * size
    for ap in (own_second, far_first):
        for b in range(ap.shape[1] // TILE):
            out_ref[pl.ds(start, ap.shape[0]), :] = ap[:, b * TILE : (b + 1) * TILE]
            start += ap.shape[0]


def pass_kernel(ref, ordered_after, out_ref):
    out_ref[...] = ref[...]


def masked_units(ref, base, flag, odd, slots, half, width, transposed):
    note = base + SLOTS * half + (META if odd else 0)
    pattern = ref[pl.ds(pl.multiple_of(note, META), META), :].astype(jnp.float32)
    pattern = pattern * jnp.where(flag, 1.0, 0.0)
    columns = []
    for i, slot in slots.items():
        tiles = []
        for a in range(half // TILE):
            k = a * width + i
            weight = jnp.broadcast_to(pattern[k : k + 1, :], (META, TILE)).astype(ref.dtype)
            tile = ref[pl.ds(pl.multiple_of(base + slot + a * TILE, META), TILE), :]
            tiles.append((tile.reshape(TILE // META, META, TILE) * weight[None]).reshape(TILE, TILE))
        columns.append(jnp.concatenate(tiles, axis=int(transposed)))
    return jnp.concatenate(columns, axis=1 - int(transposed))


def product(units, ap, transposed):
    contract = (((int(transposed),), (0,)), ((), ()))
    return lax.dot_general(units, ap, contract, preferred_element_type=jnp.float32)


def present(cols, name, kind, valid=True):
    r, c = lax.axis_index("row"), lax.axis_index("col")
    source = class_sources(r, cols)[name]
    return valid & (source >= 0) & (source < cols) & (kind_sources(c, cols)[kind] == source)


def read_applied(name, m, odd, half, size, own, far, swapped, cross_ap):
    depth, rows = 2 * half, pl.ds(m * half, half)
    if name in MAINS:
        return own[int(odd == (name == 0))][rows, :]
    if name in FARS:
        return far[int(odd == (name == 4))][rows, :]
    if odd == (name == 2):
        ref, start = swapped, len(FIRST) * size
    else:
        ref, start = cross_ap, cross_ap.shape[0] - 2 * depth
    return jnp.concatenate([ref[pl.ds(start + b * depth + m * half, half), :] for b in range(2)], axis=1)


def class_units(cols, half, width, odd, name, m, found, kinds, size, mine, theirs):
    here = [present(cols, name, kind) for kind in kinds]
    base = sum(jnp.where(flag, j * size, 0) for j, flag in enumerate(here))
    there = functools.reduce(jnp.logical_or, here)
    slots = {i: slot_of(name, i, odd, width) * half for i in found}
    ref = mine if odd == (m == 1) else theirs
    return masked_units(ref, base, there, odd, slots, half, width, True)


def kind_units(cols, half, width, odd, read, kind, ref, m):
    here = [present(cols, name, kind) for name in range(len(UNITS))]
    there = functools.reduce(jnp.logical_or, here)
    is_far = functools.reduce(jnp.logical_or, [here[name] for name in FARS])
    ap = read(0, m, odd)
    for name in range(1, len(UNITS)):
        ap = jnp.where(here[name], read(name, m, odd), ap)
    slots = {
        i: jnp.where(is_far, slot_of(FARS[0], i, odd, width), slot_of(MAINS[0], i, odd, width)) * half for i in range(width)
    }
    return masked_units(ref, 0, there, odd, slots, half, width, False), ap


def by_parity(body):
    row_odd = lax.axis_index("row") % 2 == 1
    for odd in (False, True):
        @pl.when(row_odd == odd)
        def _(odd=odd):
            body(odd)


def own_kernel(cols, half, width, own_first, own_second, swap, side, c_ref):
    size = side.shape[0]

    def body(odd):
        m = int(odd)
        units = [class_units(cols, half, width, odd, name, m, range(width), FIRST, size, swap, None) for name in MAINS]
        ap = [read_applied(name, m, odd, half, size, (own_first, own_second), None, None, None) for name in MAINS]
        c_ref[...] = product(jnp.concatenate(units, axis=1), jnp.concatenate(ap, axis=0), True)

    by_parity(body)


def near_kernel(cols, half, width, own_first, own_second, far_first, far_second, swapped, cross_ap, swap, late_first, late_second, partial, c_ref):
    size = late_first.shape[0]
    read = lambda name, m, odd: read_applied(
        name, m, odd, half, size, (own_first, own_second), (far_first, far_second), swapped, cross_ap
    )

    def body(odd):
        mine, theirs = int(odd), 1 - int(odd)
        units = lambda name, m, found: class_units(cols, half, width, odd, name, m, found, FIRST, size, swap, swapped)
        lhs = jnp.concatenate([units(name, theirs, range(width)) for name in MAINS], axis=1)
        rhs = jnp.concatenate([read(name, theirs, odd) for name in MAINS], axis=0)
        c_ref[...] = partial[...] + product(lhs, rhs, True)
        late = [
            kind_units(cols, half, width, odd, read, late_kind(step, odd), ref, mine)
            for step, ref in enumerate((late_first, late_second))
        ]
        lhs, rhs = (jnp.concatenate(x, axis=0) for x in zip(*late))
        c_ref[...] += product(lhs, rhs, False)
        for name in NEARS:
            found = sorted({i for _, i in UNITS[name]})
            lhs = jnp.concatenate([units(name, m, found) for m in range(2)], axis=1)
            rhs = jnp.concatenate([read(name, m, odd) for m in range(2)], axis=0)
            c_ref[pl.ds(found[0] * TILE, len(found) * TILE), :] += product(lhs, rhs, True)
        for name in FARS:
            for m, i in UNITS[name]:
                c_ref[pl.ds(i * TILE, TILE), :] += product(units(name, m, [i]), read(name, m, odd), True)

    by_parity(body)


def late_kernel(cols, half, width, own_first, own_second, far_first, far_second, swapped, cross_ap, late_first, partial, c_ref):
    size = late_first.shape[0]
    read = lambda name, m, odd: read_applied(
        name, m, odd, half, size, (own_first, own_second), (far_first, far_second), swapped, cross_ap
    )

    def body(odd):
        c_ref[...] = partial[...] + product(*kind_units(cols, half, width, odd, read, late_kind(0, not odd), late_first, 1 - int(odd)), False)

    by_parity(body)


def last_kernel(cols, half, width, own_first, own_second, far_first, far_second, swapped, cross_ap, late_second, partial, out_hbm, c_ref, sems):
    size = late_second.shape[0]
    read = lambda name, m, odd: read_applied(
        name, m, odd, half, size, (own_first, own_second), (far_first, far_second), swapped, cross_ap
    )

    def body(odd):
        units, ap = kind_units(cols, half, width, odd, read, late_kind(1, not odd), late_second, 1 - int(odd))
        copies = []
        for i in range(width):
            rows = pl.ds(i * TILE, TILE)
            c_ref[rows, :] = partial[rows, :] + product(units[:, i * TILE : (i + 1) * TILE], ap, False)
            copies.append(pltpu.make_async_copy(c_ref.at[rows, :], out_hbm.at[rows, :], sems.at[i]))
            copies[-1].start()
        for copy in copies:
            copy.wait()

    by_parity(body)


def on_device(rows, cols, prolong, applied, prolong_pattern, applied_pattern):
    depth, width = prolong.shape[0], prolong.shape[1] // TILE
    half = depth // 2
    data = SLOTS * half
    size = data + 2 * META
    vmem = pl.BlockSpec(memory_space=pltpu.VMEM)
    smem = pl.BlockSpec(memory_space=pltpu.SMEM)
    params = pltpu.CompilerParams(vmem_limit_bytes=24 << 20)
    shape = lambda *s: jax.ShapeDtypeStruct(s, prolong.dtype)

    def call(kernel, name, out_shape, *operands, specs=None, weight=0, **more):
        if weight:
            more["cost_estimate"] = pl.CostEstimate(flops=weight * 1_000_000_000, bytes_accessed=weight * 3_000_000, transcendentals=0)
        out_specs = (vmem,) * len(out_shape) if isinstance(out_shape, tuple) else vmem
        return pl.pallas_call(
            kernel, out_shape=out_shape, in_specs=specs or [vmem] * len(operands), out_specs=out_specs,
            compiler_params=params, name=name, **more,
        )(*operands)

    def move(x, pairs):
        return lax.ppermute(x, AXES, pairs)

    def row_pairs(pairs):
        return [(a * cols + c, b * cols + c) for a, b in pairs for c in range(cols)]

    def col_pairs(pairs):
        return [(r * cols + a, r * cols + b) for r in range(rows) for a, b in pairs if 0 <= b < cols]

    partner = row_pairs([(r, r ^ 1) for r in range(rows)])
    opposite = [(r, (r + rows // 2) % rows) for r in range(rows)]

    hbm = pl.BlockSpec(memory_space=pltpu.HBM)
    half_ap = shape(depth, applied.shape[1])
    keep, send, raw_first, raw_second = call(
        functools.partial(prepare_kernel, cols), "prepare",
        (shape(data + META, TILE),) * 2 + (shape(depth + META, applied.shape[1]),) * 2,
        *[pltpu.with_memory_space_constraint(x, pltpu.HBM) for x in (prolong, applied, prolong_pattern.T, applied_pattern.T)],
        specs=[hbm] * 4,
        scratch_shapes=[
            pltpu.VMEM(prolong.shape, prolong.dtype),
            pltpu.SMEM(prolong_pattern.shape[::-1], jnp.int32),
            pltpu.SMEM(applied_pattern.shape[::-1], jnp.int32),
            pltpu.SemaphoreType.DMA((5,)),
        ],
    )
    got = move(send, partner)
    far_first, far_second = move(raw_first, row_pairs(opposite)), move(raw_second, row_pairs(opposite))
    mine = call(merge_kernel, "merge", shape(size, TILE), keep, got)
    middle = lambda c: 2 <= c < cols - 2
    step = lambda c: c - 2 if (c // 2) % 2 == 0 else c + 2
    cross = move(mine, [
        (r * cols + c, r * cols + step(c) if middle(c) else (r ^ 1) * cols + c) for r in range(rows) for c in range(cols)
    ])
    pair = move(mine, col_pairs([(c, c ^ 2) for c in range(cols)]))
    side = move(mine, col_pairs([(c, c ^ 1) for c in range(cols)]))

    if cols == 8:
        far_pairs = [(0, 4), (1, 5), (2, 0), (3, 1), (4, 6), (5, 7), (6, 2), (7, 3)]
    else:
        far_pairs = [(c, (c + cols // 2) % cols) for c in range(cols)]
    def relay_pairs(step):
        pairs = {DIAG: [(c, c ^ 1) for c in range(cols)], FAR: far_pairs}
        return [(r * cols + a, r * cols + b) for r in range(rows) for a, b in pairs[late_kind(step, r % 2 == 1)]]

    late, after = [], cross
    for step in range(2):
        send_on = call(
            functools.partial(forward_kernel, cols, step), "forward", shape(size, TILE), mine, pair, cross, after
        )
        late.append(move(send_on, relay_pairs(step)))
        after = send_on
    own_first, own_second = call(mask_own_kernel, "mask_own", (half_ap,) * 2, raw_first, raw_second)
    far_first = call(mask_kernel, "settle_first", half_ap, far_first, mine, weight=FIRST_WEIGHT)
    swap = call(
        swap_kernel, "swap", shape(len(FIRST) * size + 4 * depth, TILE), mine, side, pair, cross, own_second, far_first
    )
    swapped = move(swap, partner)
    result = jax.ShapeDtypeStruct((prolong.shape[1], applied.shape[1]), jnp.float32)
    sizes = (cols, half, width)
    partial = call(functools.partial(own_kernel, *sizes), "own", result, own_first, own_second, swap, side)
    passed = call(pass_kernel, "pass_late", shape(size, TILE), late[0], partial)
    late_first = move(passed, partner)
    far_second = call(mask_kernel, "settle", half_ap, far_second, passed)
    late_second = move(call(pass_kernel, "pass_late", shape(size, TILE), late[1], far_second, weight=LAST_WEIGHT), partner)
    beyond = [(r, r + 1 if r % 2 == 1 else r - 1) for r in range(rows)]
    relay = [((r + rows // 2) % rows, t) for r, t in beyond if 0 <= t < rows]
    if all(h ^ 1 == t for h, t in relay):
        cross_ap = swapped
    else:
        first = own_first.reshape(depth, 2, TILE).transpose(1, 0, 2).reshape(2 * depth, TILE)
        cross_ap = move(first, row_pairs([(r, t) for r, t in beyond if 0 <= t < rows]))

    aps = (own_first, own_second, far_first, far_second, swapped, cross_ap)
    partial = call(functools.partial(near_kernel, *sizes), "near", result, *aps, swap, *late, partial)
    partial = call(functools.partial(late_kernel, *sizes), "late", result, *aps, late_first, partial)
    operands = (*aps, late_second, partial)
    return pl.pallas_call(
        functools.partial(last_kernel, *sizes), out_shape=result, in_specs=[vmem] * len(operands), out_specs=hbm,
        compiler_params=params, name="last",
        scratch_shapes=[pltpu.VMEM(result.shape, jnp.float32), pltpu.SemaphoreType.DMA((width,))],
    )(*operands)


def solution(mesh):
    in_specs = (P("col", "row"), P("row", "col"), P("col", "row"), P("row", "col"))
    return jax.shard_map(
        functools.partial(on_device, mesh.shape["row"], mesh.shape["col"]),
        mesh=mesh, in_specs=in_specs, out_specs=P("row", "col"), check_vma=False,
    )
```

```python
import functools

import jax
import jax.numpy as jnp
from jax import lax
from jax.experimental import pallas as pl
from jax.experimental.pallas import tpu as pltpu
from jax.sharding import PartitionSpec as P

TILE = 128
AXES = ("row", "col")
SIDE_WEIGHT = 2
LAST_WEIGHT, FIRST_WEIGHT = 20, 3
DIAGONAL_FIRST = 0
SLOTS = 3
META = 16
MAINS, NEARS, FARS = (0, 1), (2, 3), (4, 5)
UNITS = (
    ((0, 0), (0, 1), (0, 2), (1, 0), (1, 1), (1, 2), (1, 3)),
    ((0, 0), (0, 1), (0, 2), (0, 3), (1, 1), (1, 2), (1, 3)),
    ((0, 0), (1, 0), (1, 1)),
    ((0, 2), (0, 3), (1, 3)),
    ((0, 0), (1, 1)),
    ((0, 2), (1, 3)),
)
OWN, SIDE, PAIR, CROSS, FAR, DIAG = range(6)
FIRST, SECOND = (OWN, SIDE, PAIR, CROSS), (FAR, DIAG)


def class_sources(r, cols):
    rem = lambda x: lax.rem(x, cols)
    return (2 * r, 2 * r + 1, 2 * r - 1, 2 * r + 2, rem(2 * r + cols // 2), rem(2 * r + 1 + cols // 2))


def kind_sources(c, cols):
    even, low = c % 2 == 0, (c // 2) % 2 == 0
    near, past = jnp.where(even, c + 1, c - 1), jnp.where(even, c - 1, c + 1)
    pair, across = jnp.where(low, c + 2, c - 2), jnp.where(low, c - 2, c + 2)
    return {OWN: c, SIDE: near, PAIR: pair, CROSS: across, FAR: lax.rem(c + cols // 2, cols), DIAG: past}


def slot_of(name, i, odd, width):
    return 2 if name in FARS else (i + (width if odd else 0)) % SLOTS


def prepare_kernel(cols, p_hbm, ap_hbm, p_pattern_hbm, ap_pattern_hbm, keep_ref, send_ref, first_ref, second_ref, p_ref, p_pattern, ap_pattern, sems):
    depth = p_ref.shape[0]
    start = pl.multiple_of(jnp.where(lax.axis_index("row") % 2 == 1, depth, 0), depth)
    copies = [
        pltpu.make_async_copy(source, target, sems.at[i])
        for i, (source, target) in enumerate((
            (p_pattern_hbm, p_pattern),
            (p_hbm, p_ref),
            (ap_pattern_hbm, ap_pattern),
            (ap_hbm.at[pl.ds(start, depth), :], first_ref.at[pl.ds(0, depth), :]),
            (ap_hbm.at[pl.ds(depth - start, depth), :], second_ref.at[pl.ds(0, depth), :]),
        ))
    ]
    for copy in copies:
        copy.start()
    r, c = lax.axis_index("row"), lax.axis_index("col")
    tiles = p_ref.shape[0] // TILE // 2
    half = tiles * TILE
    width = p_ref.shape[1] // TILE
    sources = class_sources(r, cols)
    zeros = jnp.zeros((TILE, TILE), p_ref.dtype)
    line = lax.broadcasted_iota(jnp.int32, (META, TILE), 0)

    def pack(name, odd):
        for out_ref, m in ((keep_ref, int(odd)), (send_ref, 1 - int(odd))):
            for s in range(SLOTS):
                found = [i for mm, i in UNITS[name] if mm == m and slot_of(name, i, odd, width) == s]
                for a in range(tiles):
                    value, row = zeros, m * tiles + a
                    for i in found:
                        tile = p_ref[pl.ds(row * TILE, TILE), pl.ds(i * TILE, TILE)]
                        value = jnp.where(p_pattern[i, row] > 0, tile, value)
                    out_ref[pl.ds(s * half + a * TILE, TILE), :] = value

    def note(odd):
        for out_ref, m in ((keep_ref, int(odd)), (send_ref, 1 - int(odd))):
            value = jnp.zeros((META, TILE), jnp.float32)
            for a in range(tiles):
                for i in range(width):
                    value = jnp.where(line == a * width + i, p_pattern[i, m * tiles + a].astype(jnp.float32), value)
            out_ref[pl.ds(SLOTS * half, META), :] = value.astype(out_ref.dtype)

    copies[0].wait()
    copies[1].wait()
    for odd in (False, True):
        parity = (r % 2 == 1) == odd

        @pl.when(parity)
        def _(odd=odd):
            note(odd)

        for name in range(len(UNITS)):
            @pl.when(parity & (c == sources[name]))
            def _(name=name, odd=odd):
                pack(name, odd)

    @pl.when(functools.reduce(jnp.logical_and, [c != s for s in sources]))
    def _():
        for out in (keep_ref, send_ref):
            out[pl.ds(0, SLOTS * half), :] = jnp.zeros((SLOTS * half, TILE), p_ref.dtype)

    copies[2].wait()
    rows, columns = depth // TILE, first_ref.shape[1] // TILE
    shift = jnp.where(r % 2 == 1, rows, 0)
    for out_ref, low in ((first_ref, shift), (second_ref, rows - shift)):
        for b in range(columns):
            value = jnp.zeros((META, TILE), jnp.float32)
            for a in range(rows):
                value = jnp.where(line == a, ap_pattern[b, low + a].astype(jnp.float32), value)
            out_ref[pl.ds(depth, META), pl.ds(b * TILE, TILE)] = value.astype(out_ref.dtype)
    copies[3].wait()
    copies[4].wait()


def mask_applied(ref, out_ref):
    depth = out_ref.shape[0]
    pattern = ref[pl.ds(depth, META), :].astype(jnp.float32)
    for a in range(depth // TILE):
        weight = jnp.broadcast_to(pattern[a : a + 1, :], (META, out_ref.shape[1])).astype(ref.dtype)
        rows = pl.ds(a * TILE, TILE)
        out_ref[rows, :] = (ref[rows, :].reshape(TILE // META, META, -1) * weight[None]).reshape(TILE, -1)


def mask_kernel(ref, ordered_after, out_ref):
    mask_applied(ref, out_ref)


def mask_own_kernel(first_ref, second_ref, first_out, second_out):
    mask_applied(first_ref, first_out)
    mask_applied(second_ref, second_out)


def merge_kernel(keep_ref, got_ref, half_ref):
    odd = lax.axis_index("row") % 2 == 1
    size = keep_ref.shape[0] - META
    half_ref[pl.ds(0, size), :] = keep_ref[pl.ds(0, size), :] + got_ref[pl.ds(0, size), :]
    mine, theirs = keep_ref[pl.ds(size, META), :], got_ref[pl.ds(size, META), :]
    half_ref[pl.ds(size, META), :] = jnp.where(odd, theirs, mine)
    half_ref[pl.ds(size + META, META), :] = jnp.where(odd, mine, theirs)


def late_kind(step, odd):
    return DIAG if odd == (DIAGONAL_FIRST != step) else FAR


def forward_kernel(cols, step, own, pair, cross, ordered_after, out_ref):
    row_odd, c = lax.axis_index("row") % 2 == 1, lax.axis_index("col")
    diagonal = row_odd == (late_kind(step, True) == DIAG)
    by_pair = (c % 2 == 0) == ((c // 2) % 2 == 0)
    inner = (cols == 8) & (c >= 2) & (c < 6)
    from_pair = diagonal & by_pair
    from_own = jnp.logical_not(diagonal | inner)

    @pl.when(from_pair)
    def _():
        out_ref[...] = pair[...]

    @pl.when(from_own)
    def _():
        out_ref[...] = own[...]

    @pl.when(jnp.logical_not(from_pair | from_own))
    def _():
        out_ref[...] = cross[...]


def swap_kernel(own, side, pair, cross, own_second, far_first, out_ref):
    size = side.shape[0]
    for j, buffer in enumerate((own, side, pair, cross)):
        for a in range(0, size - 2 * META, TILE):
            out_ref[pl.ds(j * size + a, TILE), :] = buffer[pl.ds(a, TILE), :].T
        out_ref[pl.ds((j + 1) * size - 2 * META, 2 * META), :] = buffer[pl.ds(size - 2 * META, 2 * META), :]
    start = len(FIRST) * size
    for ap in (own_second, far_first):
        for b in range(ap.shape[1] // TILE):
            out_ref[pl.ds(start, ap.shape[0]), :] = ap[:, b * TILE : (b + 1) * TILE]
            start += ap.shape[0]


def pass_kernel(ref, ordered_after, out_ref):
    out_ref[...] = ref[...]


def masked_units(ref, base, flag, odd, slots, half, width, transposed):
    note = base + SLOTS * half + (META if odd else 0)
    pattern = ref[pl.ds(pl.multiple_of(note, META), META), :].astype(jnp.float32)
    pattern = pattern * jnp.where(flag, 1.0, 0.0)
    columns = []
    for i, slot in slots.items():
        tiles = []
        for a in range(half // TILE):
            k = a * width + i
            weight = jnp.broadcast_to(pattern[k : k + 1, :], (META, TILE)).astype(ref.dtype)
            tile = ref[pl.ds(pl.multiple_of(base + slot + a * TILE, META), TILE), :]
            tiles.append((tile.reshape(TILE // META, META, TILE) * weight[None]).reshape(TILE, TILE))
        columns.append(jnp.concatenate(tiles, axis=int(transposed)))
    return jnp.concatenate(columns, axis=1 - int(transposed))


def product(units, ap, transposed):
    contract = (((int(transposed),), (0,)), ((), ()))
    return lax.dot_general(units, ap, contract, preferred_element_type=jnp.float32)


def present(cols, name, kind, valid=True):
    r, c = lax.axis_index("row"), lax.axis_index("col")
    source = class_sources(r, cols)[name]
    return valid & (source >= 0) & (source < cols) & (kind_sources(c, cols)[kind] == source)


def read_applied(name, m, odd, half, size, own, far, swapped, cross_ap):
    depth, rows = 2 * half, pl.ds(m * half, half)
    if name in MAINS:
        return own[int(odd == (name == 0))][rows, :]
    if name in FARS:
        return far[int(odd == (name == 4))][rows, :]
    if odd == (name == 2):
        ref, start = swapped, len(FIRST) * size
    else:
        ref, start = cross_ap, cross_ap.shape[0] - 2 * depth
    return jnp.concatenate([ref[pl.ds(start + b * depth + m * half, half), :] for b in range(2)], axis=1)


def class_units(cols, half, width, odd, name, m, found, kinds, size, mine, theirs):
    here = [present(cols, name, kind) for kind in kinds]
    base = sum(jnp.where(flag, j * size, 0) for j, flag in enumerate(here))
    there = functools.reduce(jnp.logical_or, here)
    slots = {i: slot_of(name, i, odd, width) * half for i in found}
    ref = mine if odd == (m == 1) else theirs
    return masked_units(ref, base, there, odd, slots, half, width, True)


def kind_units(cols, half, width, odd, read, kind, ref, m):
    here = [present(cols, name, kind) for name in range(len(UNITS))]
    there = functools.reduce(jnp.logical_or, here)
    is_far = functools.reduce(jnp.logical_or, [here[name] for name in FARS])
    ap = read(0, m, odd)
    for name in range(1, len(UNITS)):
        ap = jnp.where(here[name], read(name, m, odd), ap)
    slots = {
        i: jnp.where(is_far, slot_of(FARS[0], i, odd, width), slot_of(MAINS[0], i, odd, width)) * half for i in range(width)
    }
    return masked_units(ref, 0, there, odd, slots, half, width, False), ap


def by_parity(body):
    row_odd = lax.axis_index("row") % 2 == 1
    for odd in (False, True):
        @pl.when(row_odd == odd)
        def _(odd=odd):
            body(odd)


def own_kernel(cols, half, width, own_first, own_second, swap, side, c_ref):
    size = side.shape[0]

    def body(odd):
        m = int(odd)
        units = [class_units(cols, half, width, odd, name, m, range(width), FIRST, size, swap, None) for name in MAINS]
        ap = [read_applied(name, m, odd, half, size, (own_first, own_second), None, None, None) for name in MAINS]
        c_ref[...] = product(jnp.concatenate(units, axis=1), jnp.concatenate(ap, axis=0), True)

    by_parity(body)


def near_kernel(cols, half, width, own_first, own_second, far_first, far_second, swapped, cross_ap, swap, late_first, late_second, partial, c_ref):
    size = late_first.shape[0]
    read = lambda name, m, odd: read_applied(
        name, m, odd, half, size, (own_first, own_second), (far_first, far_second), swapped, cross_ap
    )

    def body(odd):
        mine, theirs = int(odd), 1 - int(odd)
        units = lambda name, m, found: class_units(cols, half, width, odd, name, m, found, FIRST, size, swap, swapped)
        lhs = jnp.concatenate([units(name, theirs, range(width)) for name in MAINS], axis=1)
        rhs = jnp.concatenate([read(name, theirs, odd) for name in MAINS], axis=0)
        c_ref[...] = partial[...] + product(lhs, rhs, True)
        late = [
            kind_units(cols, half, width, odd, read, late_kind(step, odd), ref, mine)
            for step, ref in enumerate((late_first, late_second))
        ]
        lhs, rhs = (jnp.concatenate(x, axis=0) for x in zip(*late))
        c_ref[...] += product(lhs, rhs, False)
        for name in NEARS:
            found = sorted({i for _, i in UNITS[name]})
            lhs = jnp.concatenate([units(name, m, found) for m in range(2)], axis=1)
            rhs = jnp.concatenate([read(name, m, odd) for m in range(2)], axis=0)
            c_ref[pl.ds(found[0] * TILE, len(found) * TILE), :] += product(lhs, rhs, True)
        for name in FARS:
            for m, i in UNITS[name]:
                c_ref[pl.ds(i * TILE, TILE), :] += product(units(name, m, [i]), read(name, m, odd), True)

    by_parity(body)


def late_kernel(cols, half, width, own_first, own_second, far_first, far_second, swapped, cross_ap, late_first, partial, c_ref):
    size = late_first.shape[0]
    read = lambda name, m, odd: read_applied(
        name, m, odd, half, size, (own_first, own_second), (far_first, far_second), swapped, cross_ap
    )

    def body(odd):
        c_ref[...] = partial[...] + product(*kind_units(cols, half, width, odd, read, late_kind(0, not odd), late_first, 1 - int(odd)), False)

    by_parity(body)


def last_kernel(cols, half, width, own_first, own_second, far_first, far_second, swapped, cross_ap, late_second, partial, out_hbm, c_ref, sems):
    size = late_second.shape[0]
    read = lambda name, m, odd: read_applied(
        name, m, odd, half, size, (own_first, own_second), (far_first, far_second), swapped, cross_ap
    )

    def body(odd):
        units, ap = kind_units(cols, half, width, odd, read, late_kind(1, not odd), late_second, 1 - int(odd))
        copies = []
        for i in range(width):
            rows = pl.ds(i * TILE, TILE)
            c_ref[rows, :] = partial[rows, :] + product(units[:, i * TILE : (i + 1) * TILE], ap, False)
            copies.append(pltpu.make_async_copy(c_ref.at[rows, :], out_hbm.at[rows, :], sems.at[i]))
            copies[-1].start()
        for copy in copies:
            copy.wait()

    by_parity(body)


def on_device(rows, cols, prolong, applied, prolong_pattern, applied_pattern):
    depth, width = prolong.shape[0], prolong.shape[1] // TILE
    half = depth // 2
    data = SLOTS * half
    size = data + 2 * META
    vmem = pl.BlockSpec(memory_space=pltpu.VMEM)
    smem = pl.BlockSpec(memory_space=pltpu.SMEM)
    params = pltpu.CompilerParams(vmem_limit_bytes=24 << 20)
    shape = lambda *s: jax.ShapeDtypeStruct(s, prolong.dtype)

    def call(kernel, name, out_shape, *operands, specs=None, weight=0, **more):
        if weight:
            more["cost_estimate"] = pl.CostEstimate(flops=weight * 1_000_000_000, bytes_accessed=weight * 3_000_000, transcendentals=0)
        out_specs = (vmem,) * len(out_shape) if isinstance(out_shape, tuple) else vmem
        return pl.pallas_call(
            kernel, out_shape=out_shape, in_specs=specs or [vmem] * len(operands), out_specs=out_specs,
            compiler_params=params, name=name, **more,
        )(*operands)

    def move(x, pairs):
        return lax.ppermute(x, AXES, pairs)

    def row_pairs(pairs):
        return [(a * cols + c, b * cols + c) for a, b in pairs for c in range(cols)]

    def col_pairs(pairs):
        return [(r * cols + a, r * cols + b) for r in range(rows) for a, b in pairs if 0 <= b < cols]

    partner = row_pairs([(r, r ^ 1) for r in range(rows)])
    opposite = [(r, (r + rows // 2) % rows) for r in range(rows)]

    hbm = pl.BlockSpec(memory_space=pltpu.HBM)
    half_ap = shape(depth, applied.shape[1])
    keep, send, raw_first, raw_second = call(
        functools.partial(prepare_kernel, cols), "prepare",
        (shape(data + META, TILE),) * 2 + (shape(depth + META, applied.shape[1]),) * 2,
        *[pltpu.with_memory_space_constraint(x, pltpu.HBM) for x in (prolong, applied, prolong_pattern.T, applied_pattern.T)],
        specs=[hbm] * 4,
        scratch_shapes=[
            pltpu.VMEM(prolong.shape, prolong.dtype),
            pltpu.SMEM(prolong_pattern.shape[::-1], jnp.int32),
            pltpu.SMEM(applied_pattern.shape[::-1], jnp.int32),
            pltpu.SemaphoreType.DMA((5,)),
        ],
    )
    got = move(send, partner)
    far_first, far_second = move(raw_first, row_pairs(opposite)), move(raw_second, row_pairs(opposite))
    mine = call(merge_kernel, "merge", shape(size, TILE), keep, got, weight=SIDE_WEIGHT)
    middle = lambda c: 2 <= c < cols - 2
    step = lambda c: c - 2 if (c // 2) % 2 == 0 else c + 2
    cross = move(mine, [
        (r * cols + c, r * cols + step(c) if middle(c) else (r ^ 1) * cols + c) for r in range(rows) for c in range(cols)
    ])
    pair = move(mine, col_pairs([(c, c ^ 2) for c in range(cols)]))
    side = move(mine, col_pairs([(c, c ^ 1) for c in range(cols)]))

    if cols == 8:
        far_pairs = [(0, 4), (1, 5), (2, 0), (3, 1), (4, 6), (5, 7), (6, 2), (7, 3)]
    else:
        far_pairs = [(c, (c + cols // 2) % cols) for c in range(cols)]
    def relay_pairs(step):
        pairs = {DIAG: [(c, c ^ 1) for c in range(cols)], FAR: far_pairs}
        return [(r * cols + a, r * cols + b) for r in range(rows) for a, b in pairs[late_kind(step, r % 2 == 1)]]

    late, after = [], cross
    for step in range(2):
        send_on = call(
            functools.partial(forward_kernel, cols, step), "forward", shape(size, TILE), mine, pair, cross, after
        )
        late.append(move(send_on, relay_pairs(step)))
        after = send_on
    own_first, own_second = call(mask_own_kernel, "mask_own", (half_ap,) * 2, raw_first, raw_second)
    side = call(pass_kernel, "pass_side", shape(size, TILE), side, mine, weight=SIDE_WEIGHT)
    far_first = call(mask_kernel, "settle_first", half_ap, far_first, mine, weight=FIRST_WEIGHT)
    swap = call(
        swap_kernel, "swap", shape(len(FIRST) * size + 4 * depth, TILE), mine, side, pair, cross, own_second, far_first
    )
    swapped = move(swap, partner)
    result = jax.ShapeDtypeStruct((prolong.shape[1], applied.shape[1]), jnp.float32)
    sizes = (cols, half, width)
    partial = call(functools.partial(own_kernel, *sizes), "own", result, own_first, own_second, swap, side)
    passed = call(pass_kernel, "pass_late", shape(size, TILE), late[0], partial)
    late_first = move(passed, partner)
    far_second = call(mask_kernel, "settle", half_ap, far_second, passed)
    late_second = move(call(pass_kernel, "pass_late", shape(size, TILE), late[1], far_second, weight=LAST_WEIGHT), partner)
    beyond = [(r, r + 1 if r % 2 == 1 else r - 1) for r in range(rows)]
    relay = [((r + rows // 2) % rows, t) for r, t in beyond if 0 <= t < rows]
    if all(h ^ 1 == t for h, t in relay):
        cross_ap = swapped
    else:
        first = own_first.reshape(depth, 2, TILE).transpose(1, 0, 2).reshape(2 * depth, TILE)
        cross_ap = move(first, row_pairs([(r, t) for r, t in beyond if 0 <= t < rows]))

    aps = (own_first, own_second, far_first, far_second, swapped, cross_ap)
    partial = call(functools.partial(near_kernel, *sizes), "near", result, *aps, swap, *late, partial)
    partial = call(functools.partial(late_kernel, *sizes), "late", result, *aps, late_first, partial)
    operands = (*aps, late_second, partial)
    return pl.pallas_call(
        functools.partial(last_kernel, *sizes), out_shape=result, in_specs=[vmem] * len(operands), out_specs=hbm,
        compiler_params=params, name="last",
        scratch_shapes=[pltpu.VMEM(result.shape, jnp.float32), pltpu.SemaphoreType.DMA((width,))],
    )(*operands)


def solution(mesh):
    in_specs = (P("col", "row"), P("row", "col"), P("col", "row"), P("row", "col"))
    return jax.shard_map(
        functools.partial(on_device, mesh.shape["row"], mesh.shape["col"]),
        mesh=mesh, in_specs=in_specs, out_specs=P("row", "col"), check_vma=False,
    )
```

```python
import functools

import jax
import jax.numpy as jnp
from jax import lax
from jax.experimental import pallas as pl
from jax.experimental.pallas import tpu as pltpu
from jax.sharding import PartitionSpec as P

TILE = 128
AXES = ("row", "col")
LAST_WEIGHT, FIRST_WEIGHT = 20, 5
DIAGONAL_FIRST = 0
SLOTS = 3
META = 16
MAINS, NEARS, FARS = (0, 1), (2, 3), (4, 5)
UNITS = (
    ((0, 0), (0, 1), (0, 2), (1, 0), (1, 1), (1, 2), (1, 3)),
    ((0, 0), (0, 1), (0, 2), (0, 3), (1, 1), (1, 2), (1, 3)),
    ((0, 0), (1, 0), (1, 1)),
    ((0, 2), (0, 3), (1, 3)),
    ((0, 0), (1, 1)),
    ((0, 2), (1, 3)),
)
OWN, SIDE, PAIR, CROSS, FAR, DIAG = range(6)
FIRST, SECOND = (OWN, SIDE, PAIR, CROSS), (FAR, DIAG)


def class_sources(r, cols):
    rem = lambda x: lax.rem(x, cols)
    return (2 * r, 2 * r + 1, 2 * r - 1, 2 * r + 2, rem(2 * r + cols // 2), rem(2 * r + 1 + cols // 2))


def kind_sources(c, cols):
    even, low = c % 2 == 0, (c // 2) % 2 == 0
    near, past = jnp.where(even, c + 1, c - 1), jnp.where(even, c - 1, c + 1)
    pair, across = jnp.where(low, c + 2, c - 2), jnp.where(low, c - 2, c + 2)
    return {OWN: c, SIDE: near, PAIR: pair, CROSS: across, FAR: lax.rem(c + cols // 2, cols), DIAG: past}


def slot_of(name, i, odd, width):
    return 2 if name in FARS else (i + (width if odd else 0)) % SLOTS


def prepare_kernel(cols, p_hbm, ap_hbm, p_pattern_hbm, ap_pattern_hbm, keep_ref, send_ref, first_ref, second_ref, p_ref, p_pattern, ap_pattern, sems):
    depth = p_ref.shape[0]
    start = pl.multiple_of(jnp.where(lax.axis_index("row") % 2 == 1, depth, 0), depth)
    copies = [
        pltpu.make_async_copy(source, target, sems.at[i])
        for i, (source, target) in enumerate((
            (p_pattern_hbm, p_pattern),
            (p_hbm, p_ref),
            (ap_pattern_hbm, ap_pattern),
            (ap_hbm.at[pl.ds(start, depth), :], first_ref.at[pl.ds(0, depth), :]),
            (ap_hbm.at[pl.ds(depth - start, depth), :], second_ref.at[pl.ds(0, depth), :]),
        ))
    ]
    for copy in copies:
        copy.start()
    r, c = lax.axis_index("row"), lax.axis_index("col")
    tiles = p_ref.shape[0] // TILE // 2
    half = tiles * TILE
    width = p_ref.shape[1] // TILE
    sources = class_sources(r, cols)
    zeros = jnp.zeros((TILE, TILE), p_ref.dtype)
    line = lax.broadcasted_iota(jnp.int32, (META, TILE), 0)

    def pack(name, odd):
        for out_ref, m in ((keep_ref, int(odd)), (send_ref, 1 - int(odd))):
            for s in range(SLOTS):
                found = [i for mm, i in UNITS[name] if mm == m and slot_of(name, i, odd, width) == s]
                for a in range(tiles):
                    value, row = zeros, m * tiles + a
                    for i in found:
                        tile = p_ref[pl.ds(row * TILE, TILE), pl.ds(i * TILE, TILE)]
                        value = jnp.where(p_pattern[i, row] > 0, tile, value)
                    out_ref[pl.ds(s * half + a * TILE, TILE), :] = value

    def note(odd):
        for out_ref, m in ((keep_ref, int(odd)), (send_ref, 1 - int(odd))):
            value = jnp.zeros((META, TILE), jnp.float32)
            for a in range(tiles):
                for i in range(width):
                    value = jnp.where(line == a * width + i, p_pattern[i, m * tiles + a].astype(jnp.float32), value)
            out_ref[pl.ds(SLOTS * half, META), :] = value.astype(out_ref.dtype)

    copies[0].wait()
    copies[1].wait()
    for odd in (False, True):
        parity = (r % 2 == 1) == odd

        @pl.when(parity)
        def _(odd=odd):
            note(odd)

        for name in range(len(UNITS)):
            @pl.when(parity & (c == sources[name]))
            def _(name=name, odd=odd):
                pack(name, odd)

    @pl.when(functools.reduce(jnp.logical_and, [c != s for s in sources]))
    def _():
        for out in (keep_ref, send_ref):
            out[pl.ds(0, SLOTS * half), :] = jnp.zeros((SLOTS * half, TILE), p_ref.dtype)

    copies[2].wait()
    rows, columns = depth // TILE, first_ref.shape[1] // TILE
    shift = jnp.where(r % 2 == 1, rows, 0)
    for b in range(columns):
        value = jnp.zeros((META, TILE), jnp.float32)
        for a in range(2 * rows):
            row = lax.rem(shift + a, 2 * rows)
            value = jnp.where(line == a, ap_pattern[b, row].astype(jnp.float32), value)
        first_ref[pl.ds(depth, META), pl.ds(b * TILE, TILE)] = value.astype(first_ref.dtype)
    copies[3].wait()
    copies[4].wait()


def mask_applied(ref, first_ref, second, out_ref):
    depth = out_ref.shape[0]
    pattern = first_ref[pl.ds(depth, META), :].astype(jnp.float32)
    for a in range(depth // TILE):
        k = a + second * (depth // TILE)
        weight = jnp.broadcast_to(pattern[k : k + 1, :], (META, out_ref.shape[1])).astype(ref.dtype)
        rows = pl.ds(a * TILE, TILE)
        out_ref[rows, :] = (ref[rows, :].reshape(TILE // META, META, -1) * weight[None]).reshape(TILE, -1)


def mask_first_kernel(ref, ordered_after, out_ref):
    mask_applied(ref, ref, 0, out_ref)


def mask_second_kernel(ref, first_ref, ordered_after, out_ref):
    mask_applied(ref, first_ref, 1, out_ref)


def mask_own_kernel(first_ref, second_ref, first_out, second_out):
    mask_applied(first_ref, first_ref, 0, first_out)
    mask_applied(second_ref, first_ref, 1, second_out)


def merge_kernel(keep_ref, got_ref, half_ref):
    odd = lax.axis_index("row") % 2 == 1
    size = keep_ref.shape[0] - META
    half_ref[pl.ds(0, size), :] = keep_ref[pl.ds(0, size), :] + got_ref[pl.ds(0, size), :]
    mine, theirs = keep_ref[pl.ds(size, META), :], got_ref[pl.ds(size, META), :]
    half_ref[pl.ds(size, META), :] = jnp.where(odd, theirs, mine)
    half_ref[pl.ds(size + META, META), :] = jnp.where(odd, mine, theirs)


def late_kind(step, odd):
    return DIAG if odd == (DIAGONAL_FIRST != step) else FAR


def forward_kernel(cols, step, own, pair, cross, ordered_after, out_ref):
    row_odd, c = lax.axis_index("row") % 2 == 1, lax.axis_index("col")
    diagonal = row_odd == (late_kind(step, True) == DIAG)
    by_pair = (c % 2 == 0) == ((c // 2) % 2 == 0)
    inner = (cols == 8) & (c >= 2) & (c < 6)
    from_pair = diagonal & by_pair
    from_own = jnp.logical_not(diagonal | inner)

    @pl.when(from_pair)
    def _():
        out_ref[...] = pair[...]

    @pl.when(from_own)
    def _():
        out_ref[...] = own[...]

    @pl.when(jnp.logical_not(from_pair | from_own))
    def _():
        out_ref[...] = cross[...]


def swap_kernel(own, side, pair, cross, own_second, far_first, out_ref):
    size = side.shape[0]
    for j, buffer in enumerate((own, side, pair, cross)):
        for a in range(0, size - 2 * META, TILE):
            out_ref[pl.ds(j * size + a, TILE), :] = buffer[pl.ds(a, TILE), :].T
        out_ref[pl.ds((j + 1) * size - 2 * META, 2 * META), :] = buffer[pl.ds(size - 2 * META, 2 * META), :]
    start = len(FIRST) * size
    for ap in (own_second, far_first):
        for b in range(ap.shape[1] // TILE):
            out_ref[pl.ds(start, ap.shape[0]), :] = ap[:, b * TILE : (b + 1) * TILE]
            start += ap.shape[0]


def pass_kernel(ref, ordered_after, out_ref):
    out_ref[...] = ref[...]


def masked_units(ref, base, flag, odd, slots, half, width, transposed):
    note = base + SLOTS * half + (META if odd else 0)
    pattern = ref[pl.ds(pl.multiple_of(note, META), META), :].astype(jnp.float32)
    pattern = pattern * jnp.where(flag, 1.0, 0.0)
    columns = []
    for i, slot in slots.items():
        tiles = []
        for a in range(half // TILE):
            k = a * width + i
            weight = jnp.broadcast_to(pattern[k : k + 1, :], (META, TILE)).astype(ref.dtype)
            tile = ref[pl.ds(pl.multiple_of(base + slot + a * TILE, META), TILE), :]
            tiles.append((tile.reshape(TILE // META, META, TILE) * weight[None]).reshape(TILE, TILE))
        columns.append(jnp.concatenate(tiles, axis=int(transposed)))
    return jnp.concatenate(columns, axis=1 - int(transposed))


def product(units, ap, transposed):
    contract = (((int(transposed),), (0,)), ((), ()))
    return lax.dot_general(units, ap, contract, preferred_element_type=jnp.float32)


def present(cols, name, kind, valid=True):
    r, c = lax.axis_index("row"), lax.axis_index("col")
    source = class_sources(r, cols)[name]
    return valid & (source >= 0) & (source < cols) & (kind_sources(c, cols)[kind] == source)


def read_applied(name, m, odd, half, size, own, far, swapped, cross_ap):
    depth, rows = 2 * half, pl.ds(m * half, half)
    if name in MAINS:
        return own[int(odd == (name == 0))][rows, :]
    if name in FARS:
        return far[int(odd == (name == 4))][rows, :]
    if odd == (name == 2):
        ref, start = swapped, len(FIRST) * size
    else:
        ref, start = cross_ap, cross_ap.shape[0] - 2 * depth
    return jnp.concatenate([ref[pl.ds(start + b * depth + m * half, half), :] for b in range(2)], axis=1)


def class_units(cols, half, width, odd, name, m, found, kinds, size, mine, theirs):
    here = [present(cols, name, kind) for kind in kinds]
    base = sum(jnp.where(flag, j * size, 0) for j, flag in enumerate(here))
    there = functools.reduce(jnp.logical_or, here)
    slots = {i: slot_of(name, i, odd, width) * half for i in found}
    ref = mine if odd == (m == 1) else theirs
    return masked_units(ref, base, there, odd, slots, half, width, True)


def kind_units(cols, half, width, odd, read, kind, ref, m):
    here = [present(cols, name, kind) for name in range(len(UNITS))]
    there = functools.reduce(jnp.logical_or, here)
    is_far = functools.reduce(jnp.logical_or, [here[name] for name in FARS])
    ap = read(0, m, odd)
    for name in range(1, len(UNITS)):
        ap = jnp.where(here[name], read(name, m, odd), ap)
    slots = {
        i: jnp.where(is_far, slot_of(FARS[0], i, odd, width), slot_of(MAINS[0], i, odd, width)) * half for i in range(width)
    }
    return masked_units(ref, 0, there, odd, slots, half, width, False), ap


def by_parity(body):
    row_odd = lax.axis_index("row") % 2 == 1
    for odd in (False, True):
        @pl.when(row_odd == odd)
        def _(odd=odd):
            body(odd)


def own_kernel(cols, half, width, own_first, own_second, swap, side, c_ref):
    size = side.shape[0]

    def body(odd):
        m = int(odd)
        units = [class_units(cols, half, width, odd, name, m, range(width), FIRST, size, swap, None) for name in MAINS]
        ap = [read_applied(name, m, odd, half, size, (own_first, own_second), None, None, None) for name in MAINS]
        c_ref[...] = product(jnp.concatenate(units, axis=1), jnp.concatenate(ap, axis=0), True)

    by_parity(body)


def near_kernel(cols, half, width, own_first, own_second, far_first, far_second, swapped, cross_ap, swap, late_first, late_second, partial, c_ref):
    size = late_first.shape[0]
    read = lambda name, m, odd: read_applied(
        name, m, odd, half, size, (own_first, own_second), (far_first, far_second), swapped, cross_ap
    )

    def body(odd):
        mine, theirs = int(odd), 1 - int(odd)
        units = lambda name, m, found: class_units(cols, half, width, odd, name, m, found, FIRST, size, swap, swapped)
        lhs = jnp.concatenate([units(name, theirs, range(width)) for name in MAINS], axis=1)
        rhs = jnp.concatenate([read(name, theirs, odd) for name in MAINS], axis=0)
        c_ref[...] = partial[...] + product(lhs, rhs, True)
        late = [
            kind_units(cols, half, width, odd, read, late_kind(step, odd), ref, mine)
            for step, ref in enumerate((late_first, late_second))
        ]
        lhs, rhs = (jnp.concatenate(x, axis=0) for x in zip(*late))
        c_ref[...] += product(lhs, rhs, False)
        for name in NEARS:
            found = sorted({i for _, i in UNITS[name]})
            lhs = jnp.concatenate([units(name, m, found) for m in range(2)], axis=1)
            rhs = jnp.concatenate([read(name, m, odd) for m in range(2)], axis=0)
            c_ref[pl.ds(found[0] * TILE, len(found) * TILE), :] += product(lhs, rhs, True)
        for name in FARS:
            for m, i in UNITS[name]:
                c_ref[pl.ds(i * TILE, TILE), :] += product(units(name, m, [i]), read(name, m, odd), True)

    by_parity(body)


def late_kernel(cols, half, width, own_first, own_second, far_first, far_second, swapped, cross_ap, late_first, partial, c_ref):
    size = late_first.shape[0]
    read = lambda name, m, odd: read_applied(
        name, m, odd, half, size, (own_first, own_second), (far_first, far_second), swapped, cross_ap
    )

    def body(odd):
        c_ref[...] = partial[...] + product(*kind_units(cols, half, width, odd, read, late_kind(0, not odd), late_first, 1 - int(odd)), False)

    by_parity(body)


def last_kernel(cols, half, width, own_first, own_second, far_first, far_second, swapped, cross_ap, late_second, partial, out_hbm, c_ref, sems):
    size = late_second.shape[0]
    read = lambda name, m, odd: read_applied(
        name, m, odd, half, size, (own_first, own_second), (far_first, far_second), swapped, cross_ap
    )

    def body(odd):
        units, ap = kind_units(cols, half, width, odd, read, late_kind(1, not odd), late_second, 1 - int(odd))
        copies = []
        for i in range(width):
            rows = pl.ds(i * TILE, TILE)
            c_ref[rows, :] = partial[rows, :] + product(units[:, i * TILE : (i + 1) * TILE], ap, False)
            copies.append(pltpu.make_async_copy(c_ref.at[rows, :], out_hbm.at[rows, :], sems.at[i]))
            copies[-1].start()
        for copy in copies:
            copy.wait()

    by_parity(body)


def on_device(rows, cols, prolong, applied, prolong_pattern, applied_pattern):
    depth, width = prolong.shape[0], prolong.shape[1] // TILE
    half = depth // 2
    data = SLOTS * half
    size = data + 2 * META
    vmem = pl.BlockSpec(memory_space=pltpu.VMEM)
    smem = pl.BlockSpec(memory_space=pltpu.SMEM)
    params = pltpu.CompilerParams(vmem_limit_bytes=24 << 20)
    shape = lambda *s: jax.ShapeDtypeStruct(s, prolong.dtype)

    def call(kernel, name, out_shape, *operands, specs=None, weight=0, **more):
        if weight:
            more["cost_estimate"] = pl.CostEstimate(flops=weight * 1_000_000_000, bytes_accessed=weight * 3_000_000, transcendentals=0)
        out_specs = (vmem,) * len(out_shape) if isinstance(out_shape, tuple) else vmem
        return pl.pallas_call(
            kernel, out_shape=out_shape, in_specs=specs or [vmem] * len(operands), out_specs=out_specs,
            compiler_params=params, name=name, **more,
        )(*operands)

    def move(x, pairs):
        return lax.ppermute(x, AXES, pairs)

    def row_pairs(pairs):
        return [(a * cols + c, b * cols + c) for a, b in pairs for c in range(cols)]

    def col_pairs(pairs):
        return [(r * cols + a, r * cols + b) for r in range(rows) for a, b in pairs if 0 <= b < cols]

    partner = row_pairs([(r, r ^ 1) for r in range(rows)])
    opposite = [(r, (r + rows // 2) % rows) for r in range(rows)]

    hbm = pl.BlockSpec(memory_space=pltpu.HBM)
    half_ap = shape(depth, applied.shape[1])
    keep, send, raw_first, raw_second = call(
        functools.partial(prepare_kernel, cols), "prepare",
        (shape(data + META, TILE),) * 2 + (shape(depth + META, applied.shape[1]), half_ap),
        *[pltpu.with_memory_space_constraint(x, pltpu.HBM) for x in (prolong, applied, prolong_pattern.T, applied_pattern.T)],
        specs=[hbm] * 4,
        scratch_shapes=[
            pltpu.VMEM(prolong.shape, prolong.dtype),
            pltpu.SMEM(prolong_pattern.shape[::-1], jnp.int32),
            pltpu.SMEM(applied_pattern.shape[::-1], jnp.int32),
            pltpu.SemaphoreType.DMA((5,)),
        ],
    )
    got = move(send, partner)
    far_first, far_second = move(raw_first, row_pairs(opposite)), move(raw_second, row_pairs(opposite))
    mine = call(merge_kernel, "merge", shape(size, TILE), keep, got)
    middle = lambda c: 2 <= c < cols - 2
    step = lambda c: c - 2 if (c // 2) % 2 == 0 else c + 2
    cross = move(mine, [
        (r * cols + c, r * cols + step(c) if middle(c) else (r ^ 1) * cols + c) for r in range(rows) for c in range(cols)
    ])
    pair = move(mine, col_pairs([(c, c ^ 2) for c in range(cols)]))
    side = move(mine, col_pairs([(c, c ^ 1) for c in range(cols)]))

    if cols == 8:
        far_pairs = [(0, 4), (1, 5), (2, 0), (3, 1), (4, 6), (5, 7), (6, 2), (7, 3)]
    else:
        far_pairs = [(c, (c + cols // 2) % cols) for c in range(cols)]
    def relay_pairs(step):
        pairs = {DIAG: [(c, c ^ 1) for c in range(cols)], FAR: far_pairs}
        return [(r * cols + a, r * cols + b) for r in range(rows) for a, b in pairs[late_kind(step, r % 2 == 1)]]

    late, after = [], cross
    for step in range(2):
        send_on = call(
            functools.partial(forward_kernel, cols, step), "forward", shape(size, TILE), mine, pair, cross, after
        )
        late.append(move(send_on, relay_pairs(step)))
        after = send_on
    own_first, own_second = call(mask_own_kernel, "mask_own", (half_ap,) * 2, raw_first, raw_second)
    far_raw = far_first
    far_first = call(mask_first_kernel, "settle_first", half_ap, far_first, mine, weight=FIRST_WEIGHT)
    swap = call(
        swap_kernel, "swap", shape(len(FIRST) * size + 4 * depth, TILE), mine, side, pair, cross, own_second, far_first
    )
    swapped = move(swap, partner)
    result = jax.ShapeDtypeStruct((prolong.shape[1], applied.shape[1]), jnp.float32)
    sizes = (cols, half, width)
    partial = call(functools.partial(own_kernel, *sizes), "own", result, own_first, own_second, swap, side)
    far_second = call(mask_second_kernel, "settle", half_ap, far_second, far_raw, partial)
    late_first = move(call(pass_kernel, "pass_late", shape(size, TILE), late[0], mine), partner)
    late_second = move(call(pass_kernel, "pass_late", shape(size, TILE), late[1], far_second, weight=LAST_WEIGHT), partner)
    beyond = [(r, r + 1 if r % 2 == 1 else r - 1) for r in range(rows)]
    relay = [((r + rows // 2) % rows, t) for r, t in beyond if 0 <= t < rows]
    if all(h ^ 1 == t for h, t in relay):
        cross_ap = swapped
    else:
        first = own_first.reshape(depth, 2, TILE).transpose(1, 0, 2).reshape(2 * depth, TILE)
        cross_ap = move(first, row_pairs([(r, t) for r, t in beyond if 0 <= t < rows]))

    aps = (own_first, own_second, far_first, far_second, swapped, cross_ap)
    partial = call(functools.partial(near_kernel, *sizes), "near", result, *aps, swap, *late, partial)
    partial = call(functools.partial(late_kernel, *sizes), "late", result, *aps, late_first, partial)
    operands = (*aps, late_second, partial)
    return pl.pallas_call(
        functools.partial(last_kernel, *sizes), out_shape=result, in_specs=[vmem] * len(operands), out_specs=hbm,
        compiler_params=params, name="last",
        scratch_shapes=[pltpu.VMEM(result.shape, jnp.float32), pltpu.SemaphoreType.DMA((width,))],
    )(*operands)


def solution(mesh):
    in_specs = (P("col", "row"), P("row", "col"), P("col", "row"), P("row", "col"))
    return jax.shard_map(
        functools.partial(on_device, mesh.shape["row"], mesh.shape["col"]),
        mesh=mesh, in_specs=in_specs, out_specs=P("row", "col"), check_vma=False,
    )
```
